256 devices in a mesh: cont: 8 (over z), line: 8 (over y, core), scen: 4 (over x).
Axes of the slice: x: 4, y: 4, z: 8, core: 2. Of those that a mesh axis runs over, the one named last changes fastest.
Arguments:
- lodf: bfloat16 [1024, 4096], P('line', 'cont'), may hold values from -1 to 1
- flow: float32 [1024, 256], P('line', 'scen'), may hold values from -6 to 6
- out_flow: float32 [256, 4096], P('scen', 'cont'), may hold values from -6 to 6
- limits: float32 [1024], P('line'), may hold values from 0.5 to 2
- ptdf_mon: bfloat16 [1024, 2048], P('line'), may hold values from -6 to 6
- ptdf_out: bfloat16 [4096, 2048], P('cont'), may hold values from -6 to 6
- viol_cont: int32 [131072], P(('cont', 'line', 'scen')), may hold values from 0 to 511
- viol_line: int32 [131072], P(('cont', 'line', 'scen')), may hold values from 0 to 127
- viol_scen: int32 [131072], P(('cont', 'line', 'scen')), may hold values from 0 to 63
- rows_used: int32 [256], P(('cont', 'line', 'scen')), may hold values from 64 to 512, as said below
Outputs:
- worst: float32 [1024, 256], P('line', 'scen')
- schur: float32 [2048, 2048], P(('line', 'scen'))
The draws below stay inside these ranges and needn't reach their ends.
Inputs may be any that keep to these rules, and one draw needn't show every extreme that they name: `rows_used`: each device uses a leading run of its 512 slots; the counts are skewed, and some device is full.
All inputs are finite; a program needn't handle non-finite values.
Results may differ from the reference program's by a relative error of at most 0.00096.
Values may be sent and summed in bfloat16 or wider, within the bound.
No kernel may reach another device: no remote copies, remote signals or barrier semaphores. Data moves between devices by JAX's collectives and lax.ppermute only.
A program may use at most 128 MiB of HBM per device.

```python
import math
import jax
import jax.numpy as jnp
from jax import lax

K = 4096
S = 256
G = 2048
LINE_DEV = 128
ROWS_DEV = 512
L = 1024
CONT_DEV = 512
SCEN_DEV = 64
ROWS = 131072
N_LINE = 8
N_SCEN = 4
DEVICES = 256


def draw_rows_used(key, part):
    key_base = jax.random.fold_in(key, 11)
    key_full = jax.random.fold_in(key, 12)
    key_pick = jax.random.fold_in(key, 13)
    key_other = jax.random.fold_in(key, 14)
    base = jax.random.randint(key_base, (DEVICES,), ROWS_DEV // 8, ROWS_DEV // 2 + 1)
    full = jax.random.randint(key_full, (DEVICES,), 0, 8) == 0
    values = jnp.where(full, ROWS_DEV, base)
    first = jax.random.randint(key_pick, (), 0, DEVICES)
    second = (first + 1 + jax.random.randint(key_other, (), 0, DEVICES - 1)) % DEVICES
    values = values.at[first].set(ROWS_DEV)
    values = values.at[second].set(ROWS_DEV // 8)
    return values.astype(jnp.int32)


def place_ends(result, own_key, smallest, high):
    index_at = [jax.random.randint(jax.random.fold_in(own_key, axis), (), 0, length) for axis, length in enumerate(result.shape)]
    longest = result.shape.index(max(result.shape))
    beside = index_at[:longest] + [(index_at[longest] + 1) % result.shape[longest]] + index_at[longest + 1:]
    return result.at[tuple(index_at)].set(smallest).at[tuple(beside)].set(high)


def spiked(entries, key, source, target, shards_of, factor):
    def block_of(position):
        return (jnp.arange(entries.shape[position]) // (entries.shape[position] // shards_of)).reshape((-1,) + (1,) * (entries.ndim - 1 - position))

    first = jax.random.permutation(key, shards_of)[block_of(target)]
    other_side = (block_of(target) + shards_of // 2) % shards_of
    return jnp.where((block_of(source) == first) | (block_of(source) == other_side), factor * entries, entries)


def block_levels(key, extent, pieces, least, largest):
    level, own = 1.0, jax.random.fold_in(key, 6)
    for position, blocks in pieces:
        heights = jnp.exp(jax.random.uniform(jax.random.fold_in(own, position), (blocks,), jnp.float32, least / len(pieces), largest / len(pieces)))
        level = level * jnp.repeat(heights, extent[position] // blocks).reshape([-1 if axis == position else 1 for axis in range(len(extent))])
    return level


def bell_draw(own_key, dims, deviation, most, pieces=(), kind=jnp.bfloat16):
    loudness = block_levels(own_key, dims, pieces, -0.22, 0.18) if pieces else 1.0
    drawn = jax.random.normal(own_key, dims, jnp.float32) * deviation * loudness
    return jnp.minimum(jnp.maximum(drawn, -most), most).astype(kind)


def gaussian_with(rng, shape, spread, reach, split, heavy, kind=jnp.bfloat16):
    entries = spread * jax.random.normal(rng, shape, jnp.float32)
    if split:
        entries = entries * block_levels(rng, shape, split, -0.22, 0.18)
    return jnp.clip(spiked(entries, jax.random.fold_in(rng, 3), *heavy), -reach, reach).astype(kind)


def setup_inputs(seed: int = 0) -> dict:
    splits = jax.random.split(jax.random.key(seed), 11)
    lodf = jnp.clip(jax.random.uniform(splits[0], (L, K), jnp.float32, -1.0, 1.0) * block_levels(splits[0], (L, K), ((0, 8), (1, 8)), -0.4, 0.0), -1.0, 1.0).astype(jnp.bfloat16)
    flow = bell_draw(splits[1], (L, S), 1.0, 6.0, ((0, 8), (1, 4)), jnp.float32)
    out_flow = bell_draw(splits[2], (S, K), 1.0, 6.0, ((0, 4), (1, 8)), jnp.float32)
    limits = jnp.clip(jnp.exp(math.log(2.0) - 1.3862944 * jax.random.uniform(splits[3], (L,), jnp.float32) ** block_levels(splits[3], (L,), ((0, 8),), -0.2, 0.2)), 0.5, 2.0)
    ptdf_mon = gaussian_with(splits[4], (L, G), 1.0, 6.0, ((0, 8),), (0, 1, 8, 2.0))
    ptdf_out = gaussian_with(splits[5], (K, G), 1.0, 6.0, ((0, 8),), (0, 1, 8, 2.0))
    viol_cont = place_ends(jax.random.randint(splits[6], (ROWS,), 0, CONT_DEV), jax.random.fold_in(splits[6], 1), 0, CONT_DEV - 1).astype(jnp.int32)
    viol_line = place_ends(jax.random.randint(splits[7], (ROWS,), 0, LINE_DEV), jax.random.fold_in(splits[7], 1), 0, LINE_DEV - 1).astype(jnp.int32)
    viol_scen = place_ends(jax.random.randint(splits[8], (ROWS,), 0, SCEN_DEV), jax.random.fold_in(splits[8], 1), 0, SCEN_DEV - 1).astype(jnp.int32)
    rows_used = draw_rows_used(jax.random.fold_in(splits[10], 71), 0)
    return {"lodf": lodf, "flow": flow, "out_flow": out_flow, "limits": limits, "ptdf_mon": ptdf_mon, "ptdf_out": ptdf_out, "viol_cont": viol_cont, "viol_line": viol_line, "viol_scen": viol_scen, "rows_used": rows_used}


def reference(lodf, flow, out_flow, limits, ptdf_mon, ptdf_out, viol_cont, viol_line, viol_scen, rows_used):
    def screen(pair):
        lodf_block, flow_block = pair
        post = flow_block[:, :, None] + lodf_block.astype(jnp.float32)[:, None, :] * out_flow[None, :, :]
        return jnp.max(jnp.abs(post), axis=2)

    local = lax.map(screen, (lodf.reshape(L // 8, 8, K), flow.reshape(L // 8, 8, S))).reshape(L, S)
    worst = local / limits[:, None]

    def device_term(acc, device):
        cont_id = device // (N_LINE * N_SCEN)
        line_id = (device // N_SCEN) % N_LINE
        scen_id = device % N_SCEN
        start = device * ROWS_DEV
        cont_ids = lax.dynamic_slice_in_dim(viol_cont, start, ROWS_DEV) + cont_id * CONT_DEV
        line_ids = lax.dynamic_slice_in_dim(viol_line, start, ROWS_DEV) + line_id * LINE_DEV
        scen_ids = lax.dynamic_slice_in_dim(viol_scen, start, ROWS_DEV) + scen_id * SCEN_DEV
        coef = lodf[line_ids, cont_ids].astype(jnp.float32)
        rows = (ptdf_mon[line_ids].astype(jnp.float32) + coef[:, None] * ptdf_out[cont_ids].astype(jnp.float32)).astype(jnp.bfloat16)
        rows = lax.optimization_barrier(rows)
        post = flow[line_ids, scen_ids] + coef * out_flow[scen_ids, cont_ids]
        ratio = post / limits[line_ids]
        live = jnp.arange(ROWS_DEV, dtype=jnp.int32) < lax.dynamic_index_in_dim(rows_used, device, 0, keepdims=False)
        weight = jnp.where(live, 1.0 + ratio * ratio, jnp.zeros_like(ratio))
        wide = rows.astype(jnp.float32)
        scaled = (weight[:, None] * wide).astype(jnp.bfloat16)
        scaled = lax.optimization_barrier(scaled).astype(jnp.float32)
        term = jnp.dot(wide.T, scaled, precision=lax.Precision.HIGHEST, preferred_element_type=jnp.float32)
        return acc + term, None

    total, unused = lax.scan(device_term, jnp.zeros((G, G), jnp.float32), jnp.arange(DEVICES, dtype=jnp.int32))
    schur = total * (1.0 / (ROWS_DEV * DEVICES))
    return worst, schur
```

```python
import functools

import jax
import jax.numpy as jnp
from jax import lax
from jax.experimental import pallas as pl
from jax.experimental.pallas import tpu as pltpu
from jax.sharding import PartitionSpec as P


F32 = jnp.float32
BF16 = jnp.bfloat16
VMEM_LIMIT = 48 * 1024 * 1024

M_OWN = 0
M_TILE = 16
LIST = 80
BLOCK1 = 112


def iota(shape, axis):
    return lax.broadcasted_iota(jnp.int32, shape, axis)


def dot(a, b, dims):
    return lax.dot_general(a, b, (dims, ((), ())), preferred_element_type=F32)


NN = ((1,), (0,))
NT = ((1,), (1,))
TN = ((0,), (0,))


def split(x):
    high = x.astype(BF16)
    return high, (x - high.astype(F32)).astype(BF16)


def split3(x):
    high = x.astype(BF16)
    rest = x - high.astype(F32)
    mid, low = split(rest)
    return high, mid, low


def prep_kernel(pos, used, lists, lodf, flow, out_flow, limits, mon, out):
    c, q = pos[0], pos[2]
    n = lists.shape[1]
    lines, conts = lodf.shape
    scens = flow.shape[0]
    k, l, s = lists[0:1, :], lists[1:2, :], lists[2:3, :]
    is_l = iota((lines, n), 0) == l
    is_s = iota((scens, n), 0) == s
    one_l = jnp.where(is_l, 1.0, 0.0).astype(BF16)
    one_k = jnp.where(iota((conts, n), 0) == k, 1.0, 0.0).astype(BF16)
    by_k = dot(jnp.concatenate([lodf[...], *split3(out_flow[...])], axis=0), one_k, NN)
    coef = jnp.sum(jnp.where(is_l, by_k[:lines], 0.0), axis=0, keepdims=True)
    outs = by_k[lines : lines + scens] + by_k[lines + scens : lines + 2 * scens]
    outs = outs + by_k[lines + 2 * scens :]
    outs = jnp.sum(jnp.where(is_s, outs, 0.0), axis=0, keepdims=True)
    ratings = jnp.broadcast_to(limits[...], (16, lines))
    by_l = dot(jnp.concatenate([*split3(flow[...]), *split3(ratings)], axis=0), one_l, NN)
    flows = by_l[:scens] + by_l[scens : 2 * scens] + by_l[2 * scens : 3 * scens]
    flows = jnp.sum(jnp.where(is_s, flows, 0.0), axis=0, keepdims=True)
    base = 3 * scens
    rating = by_l[base : base + 1] + by_l[base + 16 : base + 17] + by_l[base + 32 : base + 33]
    ratio = (flows + coef * outs) / rating
    weight = jnp.where(iota((1, n), 1) < used[0], 1.0 + ratio * ratio, 0.0)
    mixed = weight * coef
    square = mixed * coef

    def rows16(x):
        high, mid, low = split3(x)
        zero = jnp.zeros((5, n), F32)
        eight = jnp.concatenate(
            [high.astype(F32), mid.astype(F32), low.astype(F32), zero], axis=0
        )
        return jnp.concatenate([eight, jnp.zeros((8, n), F32)], axis=0).astype(BF16)

    e_parts = dot(rows16(square), one_k, NT)
    e_sum = e_parts[0:1] + e_parts[1:2] + e_parts[2:3]
    d_parts = dot(rows16(weight), one_l, NT)
    d_sum = d_parts[0:1] + d_parts[1:2] + d_parts[2:3]

    lf = l.astype(F32)
    kh = jnp.where(k >= conts // 2, 1.0, 0.0)
    kl = k.astype(F32) - kh * (conts // 2)
    fields = [lf, kh, kl, *[p.astype(F32) for p in split(mixed)], *[p.astype(F32) for p in split(e_sum)]]
    rows = [f[:, 128 * j : 128 * j + 128] for f in fields for j in range(4)]
    rows += [p.astype(F32) for p in split(d_sum)]
    second = jnp.where(used[0] > n // 2, 1.0, 0.0)
    rows += [jnp.full((1, 128), 1.0, F32) * second, jnp.zeros((1, 128), F32)]
    table = jnp.concatenate(rows, axis=0).astype(BF16)

    own = mon[pl.ds(pl.multiple_of(q * 32, 32), 32), :]
    for t in range(16):
        top, low = own[0:16, 128 * t : 128 * t + 128], own[16:32, 128 * t : 128 * t + 128]
        out[2 * t, M_OWN : M_OWN + 16, :] = jnp.concatenate([top[:, :64], low[:, :64]], axis=1)
        out[2 * t + 1, M_OWN : M_OWN + 16, :] = jnp.concatenate([top[:, 64:], low[:, 64:]], axis=1)
    for j in range(8):
        m = lax.rem(c - j + 8, 8)
        for r in range(4):
            out[m * 4 + r, M_TILE : M_TILE + 32, :] = own[:, 256 * j : 256 * j + 128]
            out[m * 4 + r, M_TILE + 32 : M_TILE + 64, :] = own[:, 256 * j + 128 : 256 * j + 256]
    for b in range(32):
        out[b, LIST : LIST + 32, :] = table


def own_columns(got, m):
    parts = []
    for r in range(4):
        piece = got[m * 4 + r, M_OWN : M_OWN + 16, :]
        parts += [piece[:, :64], piece[:, 64:]]
    return jnp.concatenate(parts, axis=0)


def product_kernel(pos, got, out_rows, out_own, screened, sent, acc, core):
    me = pos[1]
    acc[...] = jnp.zeros_like(acc)

    def table(m, r):
        return got[m * 4 + r, LIST : LIST + 32, :].astype(F32)

    def pieces(f, j):
        l, kh, kl, v = f[j : j + 1], f[4 + j : 5 + j], f[8 + j : 9 + j], f[12 + j : 13 + j]
        lane_l = iota((128, 128), 0).astype(F32) == l
        left = jnp.concatenate(
            [jnp.where(lane_l, v * (1.0 - kh), 0.0), jnp.where(lane_l, v * kh, 0.0)], axis=0
        ).astype(BF16)
        right = jnp.where(iota((256, 128), 0).astype(F32) == kl, 1.0, 0.0).astype(BF16)
        return left, right

    def block(m, sums):
        e_sum, d_all = sums
        tables = [table(m, r) for r in range(4)]
        both = [pieces(f, j) for f in tables for j in (0, 1)]
        core[...] = dot(
            jnp.concatenate([p[0] for p in both], axis=1),
            jnp.concatenate([p[1] for p in both], axis=1),
            NT,
        )
        for r in range(4):

            @pl.when(jnp.max(tables[r][30:31, :]) > 0.5)
            def _():
                late = [pieces(tables[r], j) for j in (2, 3)]
                core[...] += dot(
                    jnp.concatenate([p[0] for p in late], axis=1),
                    jnp.concatenate([p[1] for p in late], axis=1),
                    NT,
                )

        mon = own_columns(got, m)
        mon2 = jnp.concatenate([mon, mon], axis=0)
        for h in range(2):
            high, low = split(core[128 * h : 128 * h + 128, :])
            acc[:, 256 * h : 256 * h + 256] += dot(mon2, jnp.concatenate([high, low], axis=0), TN)
        total = tables[0] + tables[1] + tables[2] + tables[3]
        e_sum = e_sum + total[20:24] + total[24:28]
        d_row = total[28:29] + total[29:30]
        d_all = jnp.where(iota((8, 128), 0) == m, d_row, d_all)
        return e_sum, d_all

    e_sum, d_all = lax.fori_loop(
        0, 8, block, (jnp.zeros((4, 128), F32), jnp.zeros((8, 128), F32))
    )
    e_row = jnp.concatenate([e_sum[j : j + 1] for j in range(4)], axis=1)
    y = acc[...] + (0.5 * e_row) * out_own[...].astype(F32)
    left = jnp.concatenate(split(y), axis=0)
    d_high, d_low = [p.astype(F32) for p in split(d_all)]
    d_both = jnp.concatenate([d_high, d_low], axis=1)
    for j in range(8):
        both = dot(left, out_rows[:, 256 * j : 256 * j + 256], NN)
        sent[lax.rem(j + me, 8), 0:64, :] = (both[:64] + both[64:]).astype(BF16)
        w_high, w_low = [p.astype(F32) for p in split(screened[8 * j : 8 * j + 8, :])]
        w_both = jnp.concatenate([w_high, w_low], axis=1)
        sent[j, 64:80, :] = jnp.concatenate([w_both, d_both], axis=0).astype(BF16)


def combine_kernel(pos, got2, got, limits, turned, direct, worst):
    q = pos[2]
    a = got2[0, 0:64, :].astype(F32)
    tail = got2[0, 64:80, :].astype(F32)
    high = tail[0:8, :128] + tail[0:8, 128:]
    d_all = tail[8:16, :128] + tail[8:16, 128:]
    for i in range(1, 8):
        a = a + got2[i, 0:64, :].astype(F32)
        tail = got2[i, 64:80, :].astype(F32)
        high = jnp.maximum(high, tail[0:8, :128] + tail[0:8, 128:])
        d_all = d_all + (tail[8:16, :128] + tail[8:16, 128:])
    worst[...] = high / limits[...]
    for r in range(4):
        turned[lax.rem(r - q + 4, 4), :, :] = a[:, 64 * r : 64 * r + 64].T
    d_cols = d_all.T
    lefts, rights = [], []
    for m in range(8):
        scaled = own_columns(got, m).astype(F32) * d_cols[:, m : m + 1]
        lefts.append(jnp.concatenate(split(scaled), axis=1))
        for r in range(4):
            rights.append(
                jnp.concatenate(
                    [
                        got[m * 4 + r, M_TILE : M_TILE + 32, :],
                        got[m * 4 + r, M_TILE + 32 : M_TILE + 64, :],
                    ],
                    axis=1,
                )
            )
    both = dot(jnp.concatenate(lefts, axis=0), jnp.concatenate(rights, axis=0), TN)
    direct[...] = a + both[:64] + both[64:]


def finish_kernel(scale, pos, t0, t1, t2, t3, direct, worst, sent):
    q = pos[2]
    columns = []
    for r in range(4):
        j = lax.rem(q - r + 4, 4)
        columns.append(
            jnp.where(
                j == 0,
                t0[...],
                jnp.where(j == 1, t1[...], jnp.where(j == 2, t2[...], t3[...])),
            )
        )
    tile = (direct[...] + jnp.concatenate(columns, axis=1)) * scale
    tail = jnp.concatenate([worst[...], worst[...]], axis=1)
    for i in range(8):
        sent[i, 0:64, :] = tile
        sent[i, 64:72, :] = tail


def place_kernel(pos, got, schur, worst):
    me = pos[1]
    for j in range(8):
        schur[:, 256 * j : 256 * j + 256] = got[lax.rem(j + me, 8), 0:64, :]
        worst[8 * j : 8 * j + 8, :] = got[j, 64:72, 0:128]


def call(kernel, name, outs, *args, scalars=1, scratch=(), cost=None):
    vmem = pl.BlockSpec(memory_space=pltpu.VMEM)
    smem = pl.BlockSpec(memory_space=pltpu.SMEM)
    many = len(outs) > 1
    specs = [vmem] * len(outs)
    shapes = [jax.ShapeDtypeStruct(s, d) for s, d in outs]
    return pl.pallas_call(
        kernel,
        name=name,
        out_shape=shapes if many else shapes[0],
        in_specs=[smem] * scalars + [vmem] * (len(args) - scalars),
        out_specs=specs if many else specs[0],
        scratch_shapes=list(scratch),
        compiler_params=pltpu.CompilerParams(vmem_limit_bytes=VMEM_LIMIT),
        cost_estimate=cost,
    )(*args)


def local(
    lodf, flow, out_flow, limits, ptdf_mon, ptdf_out, viol_cont, viol_line, viol_scen, rows_used
):
    c, m, q = lax.axis_index("cont"), lax.axis_index("line"), lax.axis_index("scen")
    n_cont, n_line, n_scen = (lax.axis_size(a) for a in ("cont", "line", "scen"))
    n_rows = viol_cont.shape[0]
    scale = 1.0 / (n_rows * n_cont * n_line * n_scen)
    pos = jnp.stack([c, m, q]).astype(jnp.int32)
    lists = jnp.stack([viol_cont, viol_line, viol_scen])
    ratings = limits.reshape(1, -1)
    flow_t = flow.T

    block1 = call(
        prep_kernel,
        "prep",
        [((32, BLOCK1, 128), BF16)],
        pos, rows_used, lists, lodf, flow_t, out_flow, ratings, ptdf_mon,
        scalars=2,
    )
    got1 = lax.all_to_all(block1, ("line", "scen"), 0, 0, tiled=True)

    wide = lodf.astype(F32)
    terms = wide[None, :, :] * out_flow[:, None, :]
    screened = jnp.maximum(
        jnp.abs(flow_t + jnp.max(terms, axis=2)), jnp.abs(flow_t + jnp.min(terms, axis=2))
    )
    own = lax.dynamic_slice_in_dim(ptdf_out, (m * n_scen + q) * 64, 64, 1).T

    block2 = call(
        product_kernel,
        "product",
        [((8, 80, 256), BF16)],
        pos, got1, ptdf_out, own, screened,
        scratch=[pltpu.VMEM((64, 512), F32), pltpu.VMEM((256, 256), F32)],
    )
    got2 = lax.all_to_all(block2, "cont", 0, 0, tiled=True)
    turned, direct, worst_part = call(
        combine_kernel,
        "combine",
        [((4, 64, 64), F32), ((64, 256), F32), ((8, 128), F32)],
        pos, got2, got1, ratings,
    )

    def place(i, j, k):
        return (i * n_line + j) * n_scen + k

    swapped = []
    for step in range(4):
        pairs = [
            (place(i, j, k), place(i, (i - j) % 8, (k + step) % 4))
            for i in range(n_cont)
            for j in range(n_line)
            for k in range(n_scen)
        ]
        swapped.append(lax.ppermute(turned[step], ("cont", "line", "scen"), pairs))
    block3 = call(
        functools.partial(finish_kernel, scale),
        "finish",
        [((8, 72, 256), F32)],
        pos, *swapped, direct, worst_part,
    )
    got3 = lax.all_to_all(block3, "cont", 0, 0, tiled=True)
    schur, worst_t = call(
        place_kernel, "place", [((64, 2048), F32), ((64, 128), F32)], pos, got3
    )
    return worst_t.T, schur


def solution(mesh):
    in_specs = (
        P("line", "cont"),
        P("line", "scen"),
        P("scen", "cont"),
        P("line"),
        P("line", None),
        P("cont", None),
        P(("cont", "line", "scen")),
        P(("cont", "line", "scen")),
        P(("cont", "line", "scen")),
        P(("cont", "line", "scen")),
    )
    out_specs = (P("line", "scen"), P(("line", "scen"), None))
    return jax.shard_map(local, mesh=mesh, in_specs=in_specs, out_specs=out_specs, check_vma=False)
```

```python
import functools

import jax
import jax.numpy as jnp
from jax import lax
from jax.experimental import pallas as pl
from jax.experimental.pallas import tpu as pltpu
from jax.sharding import Mesh
from jax.sharding import PartitionSpec as P


F32 = jnp.float32
BF16 = jnp.bfloat16
I16 = jnp.int16

M_OWN = 0
M_TILE = 32
LIST = 64
BLOCK1 = 96

TAIL2 = 128
BLOCK2 = 160

BLOCK3 = 80


def iota(shape, axis):
    return lax.broadcasted_iota(jnp.int32, shape, axis)


def dot(a, b, dims):
    return lax.dot_general(a, b, (dims, ((), ())), preferred_element_type=F32)


NN = ((1,), (0,))
NT = ((1,), (1,))
TN = ((0,), (0,))


def split(x):
    high = x.astype(BF16)
    return high, (x - high.astype(F32)).astype(BF16)


def split3(x):
    high = x.astype(BF16)
    rest = x - high.astype(F32)
    mid, low = split(rest)
    return high, mid, low


def place():
    return tuple(lax.axis_index(a) for a in ("cont", "y", "core", "scen"))


def prep_kernel(*refs):
    hbm, out, local, sems = refs[:9], refs[9], refs[10:19], refs[19]
    c, y, core, q = place()
    lines_here = pl.ds(pl.multiple_of(q * 32, 32), 32)
    copies = []
    for i, (source, target) in enumerate(zip(hbm, local)):
        source = source.at[lines_here, :] if i == 8 else source
        copies.append(pltpu.make_async_copy(source, target, sems.at[i]))
    for copy in copies:
        copy.start()
    for copy in copies[:8]:
        copy.wait()
    used, k4, l4, s4, lodf, flow, out_flow, limits, own_ref = local
    n = 512

    def row(ref):
        return jnp.concatenate([ref[j : j + 1, :] for j in range(4)], axis=1)

    k, l, s = row(k4), row(l4), row(s4)
    lines, conts = lodf.shape
    scens = flow.shape[0]
    is_l = iota((lines, n), 0) == l
    is_s = iota((scens, n), 0) == s
    one_l = jnp.where(is_l, 1.0, 0.0).astype(BF16)
    one_k = jnp.where(iota((conts, n), 0) == k, 1.0, 0.0).astype(BF16)
    by_k = dot(jnp.concatenate([lodf[...], *split3(out_flow[...])], axis=0), one_k, NN)
    coef = jnp.sum(jnp.where(is_l, by_k[:lines], 0.0), axis=0, keepdims=True)
    outs = by_k[lines : lines + scens] + by_k[lines + scens : lines + 2 * scens]
    outs = outs + by_k[lines + 2 * scens :]
    outs = jnp.sum(jnp.where(is_s, outs, 0.0), axis=0, keepdims=True)
    ratings = jnp.broadcast_to(limits[...], (16, lines))
    by_l = dot(jnp.concatenate([*split3(flow[...]), *split3(ratings)], axis=0), one_l, NN)
    flows = by_l[:scens] + by_l[scens : 2 * scens] + by_l[2 * scens : 3 * scens]
    flows = jnp.sum(jnp.where(is_s, flows, 0.0), axis=0, keepdims=True)
    base = 3 * scens
    rating = by_l[base : base + 1] + by_l[base + 16 : base + 17] + by_l[base + 32 : base + 33]
    ratio = (flows + coef * outs) / rating
    weight = jnp.where(iota((1, n), 1) < used[0], 1.0 + ratio * ratio, 0.0)
    mixed = weight * coef
    square = mixed * coef

    def rows16(x):
        parts = [p.astype(F32) for p in split3(x)]
        return jnp.concatenate([*parts, jnp.zeros((13, n), F32)], axis=0).astype(BF16)

    e_parts = dot(rows16(square), one_k, NT)
    e_sum = e_parts[0:1] + e_parts[1:2] + e_parts[2:3]
    d_parts = dot(rows16(weight), one_l, NT)
    d_sum = d_parts[0:1] + d_parts[1:2] + d_parts[2:3]

    upper = k >= conts // 2
    kl = jnp.where(upper, k - conts // 2, k)
    fields = [
        l.astype(F32),
        kl.astype(F32),
        jnp.where(upper, 0.0, mixed),
        jnp.where(upper, mixed, 0.0),
        *[p.astype(F32) for p in split(e_sum)],
    ]
    rows = [f[:, 128 * j : 128 * j + 128] for f in fields for j in range(4)]
    rows += [p.astype(F32) for p in split(d_sum)]
    rows += [jnp.full((1, 128), jnp.where(used[0] > n // 2, 1.0, 0.0), F32)]
    rows += [jnp.zeros((32 - len(rows), 128), F32)]
    table = jnp.concatenate(rows, axis=0).astype(BF16)
    for b in range(32):
        out[b, LIST : LIST + 32, :] = table

    copies[8].wait()
    own = own_ref[...]
    t_y, t_q = core * 2 + c // 4, c % 4
    for yy in range(4):
        for qq in range(4):
            first = 512 * yy + 64 * qq
            part = jnp.concatenate(
                [own[:, first : first + 64], own[:, first + 256 : first + 320]], axis=1
            )
            for cc in range(2):
                out[(yy * 2 + cc) * 4 + qq, M_OWN : M_OWN + 32, :] = part
                to_y = lax.bitwise_xor(jnp.int32(yy), 2 * cc + c // 4)
                to_q = lax.bitwise_xor(jnp.int32(qq), t_q)
                out[(to_y * 2 + cc) * 4 + to_q, M_TILE : M_TILE + 32, :] = part


def product_kernel(got, out_rows, own_t, screened, sent, acc, core_ref):
    c, y, core, q = place()
    acc[...] = jnp.zeros_like(acc)

    def pieces(f, j):
        l, kl, low, up = f[j : j + 1], f[4 + j : 5 + j], f[8 + j : 9 + j], f[12 + j : 13 + j]
        is_l = iota((128, 128), 0).astype(F32) == l
        left = jnp.concatenate(
            [jnp.where(is_l, low, 0.0), jnp.where(is_l, up, 0.0)], axis=0
        ).astype(BF16)
        right = jnp.where(iota((256, 128), 0).astype(F32) == kl, 1.0, 0.0).astype(BF16)
        return left, right

    def pair(parts):
        return (
            jnp.concatenate([p[0] for p in parts], axis=1),
            jnp.concatenate([p[1] for p in parts], axis=1),
        )

    def block(m, sums):
        e_sum, d_all = sums
        tables = [got[m * 4 + r, LIST : LIST + 32, :].astype(F32) for r in range(4)]
        core_ref[...] = dot(*pair([pieces(f, j) for f in tables for j in (0, 1)]), NT)
        for r in range(4):

            @pl.when(jnp.max(tables[r][26:27, :]) > 0.5)
            def _():
                core_ref[...] += dot(*pair([pieces(tables[r], j) for j in (2, 3)]), NT)

        mon = jnp.concatenate([got[m * 4 + r, M_OWN : M_OWN + 32, :] for r in range(4)], axis=0)
        mon2 = jnp.concatenate([mon, mon], axis=0)
        for h in range(2):
            high, low = split(core_ref[128 * h : 128 * h + 128, :])
            acc[:, 256 * h : 256 * h + 256] += dot(mon2, jnp.concatenate([high, low], axis=0), TN)
        total = tables[0] + tables[1] + tables[2] + tables[3]
        e_sum = e_sum + total[16:20] + total[20:24]
        d_all = jnp.where(iota((8, 128), 0) == m, total[24:25] + total[25:26], d_all)
        return e_sum, d_all

    e_sum, d_all = lax.fori_loop(
        0, 8, block, (jnp.zeros((4, 128), F32), jnp.zeros((8, 128), F32))
    )
    e_row = jnp.concatenate([e_sum[j : j + 1] for j in range(4)], axis=1)
    part = acc[...] + (0.5 * e_row) * own_t[...].astype(F32)
    left = jnp.concatenate(split(part), axis=0)
    d_rows = [p.astype(F32) for p in split(d_all)]
    for i in range(8):
        w_rows = [p.astype(F32) for p in split(screened[8 * i : 8 * i + 8, :])]
        sent[i, TAIL2:BLOCK2, :] = jnp.concatenate([*w_rows, *d_rows], axis=0).astype(BF16)
    half = lax.bitwise_xor(y // 2, core)
    columns = out_rows[:, pl.ds(pl.multiple_of(half * 1024, 1024), 1024)]
    for yy in range(2):
        both = dot(left, columns[:, 512 * yy : 512 * yy + 512], NN)
        tile = (both[:128] + both[128:]).astype(BF16)
        for qq in range(4):
            to = lax.bitwise_xor(jnp.int32(yy), y % 2) * 4 + lax.bitwise_xor(jnp.int32(qq), q)
            sent[to, 0:128, :] = jnp.concatenate(
                [tile[:, 64 * qq : 64 * qq + 64], tile[:, 256 + 64 * qq : 320 + 64 * qq]], axis=1
            )


def combine_kernel(got2, got, limits, turned, direct, worst):
    a = got2[0, 0:128, :].astype(F32)
    tail = got2[0, TAIL2:BLOCK2, :].astype(F32)
    high = tail[0:8] + tail[8:16]
    d_all = tail[16:24] + tail[24:32]
    for i in range(1, 8):
        a = a + got2[i, 0:128, :].astype(F32)
        tail = got2[i, TAIL2:BLOCK2, :].astype(F32)
        high = jnp.maximum(high, tail[0:8] + tail[8:16])
        d_all = d_all + (tail[16:24] + tail[24:32])
    worst[...] = high / limits[...]
    turned[...] = a.T
    d_cols = d_all.T
    lefts, rights = [], []
    for m in range(8):
        mon = jnp.concatenate([got[m * 4 + r, M_OWN : M_OWN + 32, :] for r in range(4)], axis=0)
        lefts.append(jnp.concatenate(split(mon.astype(F32) * d_cols[:, m : m + 1]), axis=1))
        rights += [got[m * 4 + r, M_TILE : M_TILE + 32, :] for r in range(4)]
    both = dot(jnp.concatenate(lefts, axis=0), jnp.concatenate(rights, axis=0), TN)
    direct[...] = a + both[:128] + both[128:]


def encode(x):
    top = jnp.maximum(jnp.max(jnp.abs(x), axis=0, keepdims=True), 1e-30)
    exponent = jnp.floor(jnp.log2(top) + 1.001) - 15.0
    return jnp.floor(x * jnp.exp2(-exponent) + 0.5), exponent


def finish_kernel(scale, turned, direct, worst, sent):
    tile = (direct[...] + turned[...]) * scale
    worst_code, worst_exp = encode(worst[...])
    for core in range(2):
        code, exp = encode(tile[64 * core : 64 * core + 64, :])
        rows = [code, worst_code, exp, worst_exp, jnp.zeros((BLOCK3 - 74, 128), F32)]
        block = jnp.concatenate(rows, axis=0).astype(jnp.int32).astype(I16)
        for i in range(8):
            sent[2 * i + core, :, :] = block


def decode(code, exponent):
    return code * jnp.exp2(exponent)


def place_kernel(got, schur, worst):
    c, y, core, q = place()
    for yy in range(4):
        parts = []
        for qq in range(4):
            source_c = lax.bitwise_xor(jnp.int32(yy % 2), y % 2) * 4
            source_c = source_c + lax.bitwise_xor(jnp.int32(qq), q)
            source_core = lax.bitwise_xor(jnp.int32(yy // 2), y // 2)
            block = got[source_c * 2 + source_core, :, :].astype(jnp.int32).astype(F32)
            parts.append(decode(block[0:64], block[72:73]))
        schur[:, 512 * yy : 512 * yy + 512] = jnp.concatenate(
            [p[:, :64] for p in parts] + [p[:, 64:] for p in parts], axis=1
        )
    for i in range(8):
        block = got[2 * i + core, 64:80, :].astype(jnp.int32).astype(F32)
        worst[8 * i : 8 * i + 8, :] = decode(block[0:8], block[9:10])


def call(kernel, name, outs, *args, scratch=(), space=pltpu.VMEM, vmem_mib=24):
    vmem = pl.BlockSpec(memory_space=pltpu.VMEM)
    specs = [vmem] * len(outs)
    shapes = [jax.ShapeDtypeStruct(s, d) for s, d in outs]
    many = len(outs) > 1
    return pl.pallas_call(
        kernel,
        name=name,
        out_shape=shapes if many else shapes[0],
        in_specs=[pl.BlockSpec(memory_space=space)] * len(args),
        out_specs=specs if many else specs[0],
        scratch_shapes=list(scratch),
        compiler_params=pltpu.CompilerParams(vmem_limit_bytes=vmem_mib * 1024 * 1024),
    )(*args)


PLANE = ("y", "core", "scen")
EVERY = ("cont", "y", "core", "scen")


def local(
    lodf, flow, out_flow, limits, ptdf_mon, ptdf_out, viol_cont, viol_line, viol_scen, rows_used
):
    sizes = [lax.axis_size(a) for a in EVERY]
    n_rows = viol_cont.shape[0]
    scale = 1.0 / (n_rows * sizes[0] * sizes[1] * sizes[2] * sizes[3])
    ratings = limits.reshape(1, -1)
    flow_t = flow.T

    inputs = [
        rows_used,
        viol_cont.reshape(4, 128),
        viol_line.reshape(4, 128),
        viol_scen.reshape(4, 128),
        lodf,
        flow_t,
        out_flow,
        ratings,
        ptdf_mon,
    ]
    scratch = [pltpu.SMEM(rows_used.shape, jnp.int32)]
    scratch += [pltpu.VMEM(a.shape, a.dtype) for a in inputs[1:8]]
    scratch += [pltpu.VMEM((32, ptdf_mon.shape[1]), BF16), pltpu.SemaphoreType.DMA((9,))]
    block1 = call(
        prep_kernel, "prep", [((32, BLOCK1, 128), BF16)], *inputs, scratch=scratch, space=pl.ANY, vmem_mib=60
    )
    got1 = lax.all_to_all(block1, PLANE, 0, 0, tiled=True)

    wide = lodf.astype(F32)
    terms = wide[None, :, :] * out_flow[:, None, :]
    screened = jnp.maximum(
        jnp.abs(flow_t + jnp.max(terms, axis=2)), jnp.abs(flow_t + jnp.min(terms, axis=2))
    )
    first = 512 * lax.axis_index("y") + 64 * lax.axis_index("scen")
    own_t = jnp.concatenate(
        [lax.dynamic_slice_in_dim(ptdf_out, first + 256 * i, 64, 1) for i in range(2)], axis=1
    ).T

    block2 = call(
        product_kernel,
        "product",
        [((8, BLOCK2, 128), BF16)],
        got1, ptdf_out, own_t, screened,
        scratch=[pltpu.VMEM((128, 512), F32), pltpu.VMEM((256, 256), F32)],
    )
    got2 = lax.all_to_all(block2, "cont", 0, 0, tiled=True)
    turned, direct, worst_part = call(
        combine_kernel,
        "combine",
        [((128, 128), F32), ((128, 128), F32), ((8, 128), F32)],
        got2, got1, ratings,
    )

    def index(c, y, core, q):
        return ((c * sizes[1] + y) * sizes[2] + core) * sizes[3] + q

    pairs = [
        (index(c, y, core, q), index(c, y ^ (core * 2 + c // 4), core, q ^ (c % 4)))
        for c in range(sizes[0])
        for y in range(sizes[1])
        for core in range(sizes[2])
        for q in range(sizes[3])
    ]
    turned = lax.ppermute(turned, EVERY, pairs)
    block3 = call(
        functools.partial(finish_kernel, scale),
        "finish",
        [((16, BLOCK3, 128), I16)],
        turned, direct, worst_part,
    )
    got3 = lax.all_to_all(block3, ("cont", "core"), 0, 0, tiled=True)
    schur, worst_t = call(
        place_kernel, "place", [((64, 2048), F32), ((64, 128), F32)], got3
    )
    return worst_t.T, schur


def solution(mesh):
    n_cont, n_line, n_scen = (mesh.shape[a] for a in ("cont", "line", "scen"))
    fine = Mesh(mesh.devices.reshape(n_cont, n_line // 2, 2, n_scen), EVERY)
    line = ("y", "core")
    every = P(EVERY)
    in_specs = (
        P(line, "cont"),
        P(line, "scen"),
        P("scen", "cont"),
        P(line),
        P(line, None),
        P("cont", None),
        every,
        every,
        every,
        every,
    )
    out_specs = (P(line, "scen"), P((*line, "scen"), None))
    return jax.shard_map(local, mesh=fine, in_specs=in_specs, out_specs=out_specs, check_vma=False)
```

```python
import functools

import jax
import jax.numpy as jnp
from jax import lax
from jax.experimental import pallas as pl
from jax.experimental.pallas import tpu as pltpu
from jax.sharding import Mesh
from jax.sharding import PartitionSpec as P


F32 = jnp.float32
BF16 = jnp.bfloat16
I16 = jnp.int16

M_OWN = 0
M_TILE = 32
LIST = 64
BLOCK1 = 96

TAIL2 = 128
BLOCK2 = 160

BLOCK3 = 80


def iota(shape, axis):
    return lax.broadcasted_iota(jnp.int32, shape, axis)


def dot(a, b, dims):
    return lax.dot_general(a, b, (dims, ((), ())), preferred_element_type=F32)


NN = ((1,), (0,))
NT = ((1,), (1,))
TN = ((0,), (0,))


def split(x):
    high = x.astype(BF16)
    return high, (x - high.astype(F32)).astype(BF16)


def split3(x):
    high = x.astype(BF16)
    rest = x - high.astype(F32)
    mid, low = split(rest)
    return high, mid, low


def place():
    return tuple(lax.axis_index(a) for a in ("cont", "y", "core", "scen"))


def prep_kernel(*refs):
    hbm, out, local, sems = refs[:9], refs[9], refs[10:19], refs[19]
    c, y, core, q = place()
    lines_here = pl.ds(pl.multiple_of(q * 32, 32), 32)
    copies = []
    for i, (source, target) in enumerate(zip(hbm, local)):
        source = source.at[lines_here, :] if i == 8 else source
        copies.append(pltpu.make_async_copy(source, target, sems.at[i]))
    for copy in copies:
        copy.start()
    for copy in copies:
        copy.wait()
    used, k4, l4, s4, lodf, flow, out_flow, limits, own_ref = local
    n = 512

    def row(ref):
        return jnp.concatenate([ref[j : j + 1, :] for j in range(4)], axis=1)

    k, l, s = row(k4), row(l4), row(s4)
    lines, conts = lodf.shape
    scens = flow.shape[0]
    is_l = iota((lines, n), 0) == l
    is_s = iota((scens, n), 0) == s
    one_l = jnp.where(is_l, 1.0, 0.0).astype(BF16)
    one_k = jnp.where(iota((conts, n), 0) == k, 1.0, 0.0).astype(BF16)
    by_k = dot(jnp.concatenate([lodf[...], *split3(out_flow[...])], axis=0), one_k, NN)
    coef = jnp.sum(jnp.where(is_l, by_k[:lines], 0.0), axis=0, keepdims=True)
    outs = by_k[lines : lines + scens] + by_k[lines + scens : lines + 2 * scens]
    outs = outs + by_k[lines + 2 * scens :]
    outs = jnp.sum(jnp.where(is_s, outs, 0.0), axis=0, keepdims=True)
    ratings = jnp.broadcast_to(limits[...], (16, lines))
    by_l = dot(jnp.concatenate([*split3(flow[...]), *split3(ratings)], axis=0), one_l, NN)
    flows = by_l[:scens] + by_l[scens : 2 * scens] + by_l[2 * scens : 3 * scens]
    flows = jnp.sum(jnp.where(is_s, flows, 0.0), axis=0, keepdims=True)
    base = 3 * scens
    rating = by_l[base : base + 1] + by_l[base + 16 : base + 17] + by_l[base + 32 : base + 33]
    ratio = (flows + coef * outs) / rating
    weight = jnp.where(iota((1, n), 1) < used[0], 1.0 + ratio * ratio, 0.0)
    mixed = weight * coef
    square = mixed * coef

    def rows16(x):
        parts = [p.astype(F32) for p in split3(x)]
        return jnp.concatenate([*parts, jnp.zeros((13, n), F32)], axis=0).astype(BF16)

    e_parts = dot(rows16(square), one_k, NT)
    e_sum = e_parts[0:1] + e_parts[1:2] + e_parts[2:3]
    d_parts = dot(rows16(weight), one_l, NT)
    d_sum = d_parts[0:1] + d_parts[1:2] + d_parts[2:3]

    upper = k >= conts // 2
    kl = jnp.where(upper, k - conts // 2, k)
    fields = [
        l.astype(F32),
        kl.astype(F32),
        jnp.where(upper, 0.0, mixed),
        jnp.where(upper, mixed, 0.0),
        *[p.astype(F32) for p in split(e_sum)],
    ]
    rows = [f[:, 128 * j : 128 * j + 128] for f in fields for j in range(4)]
    rows += [p.astype(F32) for p in split(d_sum)]
    rows += [jnp.zeros((32 - len(rows), 128), F32)]
    table = jnp.concatenate(rows, axis=0).astype(BF16)
    for b in range(16):
        out[b, LIST : LIST + 32, :] = table

    own = own_ref[...]
    for yy in range(4):
        for qq in range(4):
            first = 512 * yy + 64 * qq
            part = jnp.concatenate(
                [own[:, first : first + 64], own[:, first + 256 : first + 320]], axis=1
            )
            out[yy * 4 + qq, M_OWN : M_OWN + 32, :] = part
            for cc in range(2):
                to_y = lax.bitwise_xor(jnp.int32(yy), 2 * cc + c // 4)
                to = to_y * 4 + lax.bitwise_xor(jnp.int32(qq), c % 4)
                lines = jnp.where(to < yy * 4 + qq, part[0:16].astype(F32), part[16:32].astype(F32))
                first_row = M_TILE + 16 * cc
                out[to, first_row : first_row + 16, :] = lines.astype(BF16)


def half_product(got):
    def pieces(f, j):
        l, kl, low, up = f[j : j + 1], f[4 + j : 5 + j], f[8 + j : 9 + j], f[12 + j : 13 + j]
        is_l = iota((128, 128), 0).astype(F32) == l
        left = jnp.concatenate(
            [jnp.where(is_l, low, 0.0), jnp.where(is_l, up, 0.0)], axis=0
        ).astype(BF16)
        right = jnp.where(iota((256, 128), 0).astype(F32) == kl, 1.0, 0.0).astype(BF16)
        return left, right

    e_sum, d_rows, cores = jnp.zeros((8, 128), F32), [], []
    for yy in range(4):
        tables = [got[yy * 4 + r, LIST : LIST + 32, :].astype(F32) for r in range(4)]
        both = [pieces(f, j) for f in tables for j in range(4)]
        core = dot(
            jnp.concatenate([p[0] for p in both], axis=1),
            jnp.concatenate([p[1] for p in both], axis=1),
            NT,
        )
        cores.append(jnp.concatenate([core[:128], core[128:]], axis=1))
        total = tables[0] + tables[1] + tables[2] + tables[3]
        e_sum = e_sum + total[16:24]
        d_rows.append(total[24:25] + total[25:26])
    mon = jnp.concatenate([got[i, M_OWN : M_OWN + 32, :] for i in range(16)], axis=0)
    high, low = split(jnp.concatenate(cores, axis=0))
    part = dot(mon, high, TN) + dot(mon, low, TN)
    return part, jnp.concatenate([e_sum[0:4] + e_sum[4:8], *d_rows], axis=0)


def first_kernel(got, part, sums):
    part[...], sums[...] = half_product(got)


def second_kernel(got, part1, sums1, out_rows, own_t, screened, sent):
    c, y, core, q = place()
    part, sums = half_product(got)
    e_sum = sums1[0:4, :] + sums[0:4]
    e_row = jnp.concatenate([e_sum[j : j + 1] for j in range(4)], axis=1)
    part = part1[...] + part + (0.5 * e_row) * own_t[...].astype(F32)
    left = jnp.concatenate(split(part), axis=0)
    d_all = jnp.concatenate([sums1[4:8, :], sums[4:8]], axis=0)
    d_rows = [p.astype(F32) for p in split(d_all)]
    for i in range(8):
        w_rows = [p.astype(F32) for p in split(screened[8 * i : 8 * i + 8, :])]
        sent[i, TAIL2:BLOCK2, :] = jnp.concatenate([*w_rows, *d_rows], axis=0).astype(BF16)
    half = lax.bitwise_xor(y // 2, core)
    for yy in range(2):
        first = pl.multiple_of(half * 1024 + 512 * yy, 512)
        both = dot(left, out_rows[:, pl.ds(first, 512)], NN)
        tile = (both[:128] + both[128:]).astype(BF16)
        for qq in range(4):
            to = lax.bitwise_xor(jnp.int32(yy), y % 2) * 4 + lax.bitwise_xor(jnp.int32(qq), q)
            sent[to, 0:128, :] = jnp.concatenate(
                [tile[:, 64 * qq : 64 * qq + 64], tile[:, 256 + 64 * qq : 320 + 64 * qq]], axis=1
            )


def combine_kernel(got2, own, other, limits, turned, direct, worst, d_ref):
    c, y, core, q = place()
    a = got2[0, 0:128, :].astype(F32)
    tail = got2[0, TAIL2:BLOCK2, :].astype(F32)
    high = tail[0:8] + tail[8:16]
    d_all = tail[16:24] + tail[24:32]
    for i in range(1, 8):
        a = a + got2[i, 0:128, :].astype(F32)
        tail = got2[i, TAIL2:BLOCK2, :].astype(F32)
        high = jnp.maximum(high, tail[0:8] + tail[8:16])
        d_all = d_all + (tail[16:24] + tail[24:32])
    worst[...] = high / limits[...]
    d_ref[...] = d_all.T

    def side(h):
        lefts = []
        for i, got in enumerate((own, other)):
            for yy in range(4):
                for r in range(4):
                    lines = pl.ds(pl.multiple_of(32 * r + 16 * h, 16), 16)
                    mon = got[yy * 4 + r, pl.ds(pl.multiple_of(M_OWN + 16 * h, 16), 16), :]
                    scaled = mon.astype(F32) * d_ref[lines, 4 * i + yy : 4 * i + yy + 1]
                    lefts.append(jnp.concatenate(split(scaled), axis=1))
        return jnp.concatenate(lefts, axis=0)

    def write(both, factor):
        total = a + factor * (both[:128] + both[128:])
        direct[...] = total
        turned[...] = total.T

    alone = (c == 0) & (core == 0)

    @pl.when(alone)
    def _():
        both = 0.0
        for h in range(2):
            rights = [g[i, M_OWN + 16 * h : M_OWN + 16 * h + 16, :] for g in (own, other) for i in range(16)]
            both = both + dot(side(h), jnp.concatenate(rights, axis=0), TN)
        write(both, 0.5)

    @pl.when(jnp.logical_not(alone))
    def _():
        to_y = lax.bitwise_xor(y, 2 * core + c // 4)
        to_q = lax.bitwise_xor(q, c % 4)
        h = jnp.where(y * 4 + q < to_y * 4 + to_q, 0, 1)
        there = pl.ds(pl.multiple_of(M_TILE + 16 * core, 16), 16)
        rights = [g[i, there, :] for g in (own, other) for i in range(16)]
        write(dot(side(h), jnp.concatenate(rights, axis=0), TN), 1.0)


def encode(x):
    top = jnp.maximum(jnp.max(jnp.abs(x), axis=0, keepdims=True), 1e-30)
    exponent = jnp.floor(jnp.log2(top) + 1.001) - 15.0
    return jnp.floor(x * jnp.exp2(-exponent) + 0.5), exponent


def finish_kernel(scale, turned, direct, worst, sent):
    tile = (direct[...] + turned[...]) * scale
    worst_code, worst_exp = encode(worst[...])
    for core in range(2):
        code, exp = encode(tile[64 * core : 64 * core + 64, :])
        rows = [code, worst_code, exp, worst_exp, jnp.zeros((BLOCK3 - 74, 128), F32)]
        block = jnp.concatenate(rows, axis=0).astype(jnp.int32).astype(I16)
        for i in range(8):
            sent[2 * i + core, :, :] = block


def decode(code, exponent):
    return code * jnp.exp2(exponent)


def place_kernel(got, schur, worst):
    c, y, core, q = place()
    for yy in range(4):
        parts = []
        for qq in range(4):
            source_c = lax.bitwise_xor(jnp.int32(yy % 2), y % 2) * 4
            source_c = source_c + lax.bitwise_xor(jnp.int32(qq), q)
            source_core = lax.bitwise_xor(jnp.int32(yy // 2), y // 2)
            block = got[source_c * 2 + source_core, :, :].astype(jnp.int32).astype(F32)
            parts.append(decode(block[0:64], block[72:73]))
        schur[:, 512 * yy : 512 * yy + 512] = jnp.concatenate(
            [p[:, :64] for p in parts] + [p[:, 64:] for p in parts], axis=1
        )
    for i in range(8):
        block = got[2 * i + core, 64:80, :].astype(jnp.int32).astype(F32)
        worst[8 * i : 8 * i + 8, :] = decode(block[0:8], block[9:10])


def call(kernel, name, outs, *args, scratch=(), space=pltpu.VMEM, vmem_mib=24):
    vmem = pl.BlockSpec(memory_space=pltpu.VMEM)
    specs = [vmem] * len(outs)
    shapes = [jax.ShapeDtypeStruct(s, d) for s, d in outs]
    many = len(outs) > 1
    return pl.pallas_call(
        kernel,
        name=name,
        out_shape=shapes if many else shapes[0],
        in_specs=[pl.BlockSpec(memory_space=space)] * len(args),
        out_specs=specs if many else specs[0],
        scratch_shapes=list(scratch),
        compiler_params=pltpu.CompilerParams(vmem_limit_bytes=vmem_mib * 1024 * 1024),
    )(*args)


EVERY = ("cont", "y", "core", "scen")


def local(
    lodf, flow, out_flow, limits, ptdf_mon, ptdf_out, viol_cont, viol_line, viol_scen, rows_used
):
    sizes = [lax.axis_size(a) for a in EVERY]
    n_rows = viol_cont.shape[0]
    scale = 1.0 / (n_rows * sizes[0] * sizes[1] * sizes[2] * sizes[3])
    ratings = limits.reshape(1, -1)
    flow_t = flow.T

    inputs = [
        rows_used,
        viol_cont.reshape(4, 128),
        viol_line.reshape(4, 128),
        viol_scen.reshape(4, 128),
        lodf,
        flow_t,
        out_flow,
        ratings,
        ptdf_mon,
    ]
    scratch = [pltpu.SMEM(rows_used.shape, jnp.int32)]
    scratch += [pltpu.VMEM(a.shape, a.dtype) for a in inputs[1:8]]
    scratch += [pltpu.VMEM((32, ptdf_mon.shape[1]), BF16), pltpu.SemaphoreType.DMA((9,))]
    block1 = call(
        prep_kernel, "prep", [((16, BLOCK1, 128), BF16)], *inputs, scratch=scratch, space=pl.ANY, vmem_mib=60
    )
    got1 = lax.all_to_all(block1, ("y", "scen"), 0, 0, tiled=True)
    other1 = lax.ppermute(got1, "core", [(0, 1), (1, 0)])

    wide = lodf.astype(F32)
    terms = wide[None, :, :] * out_flow[:, None, :]
    screened = jnp.maximum(
        jnp.abs(flow_t + jnp.max(terms, axis=2)), jnp.abs(flow_t + jnp.min(terms, axis=2))
    )
    first = 512 * lax.axis_index("y") + 64 * lax.axis_index("scen")
    own_t = jnp.concatenate(
        [lax.dynamic_slice_in_dim(ptdf_out, first + 256 * i, 64, 1) for i in range(2)], axis=1
    ).T

    part, sums = call(first_kernel, "first", [((128, 512), F32), ((8, 128), F32)], got1)
    block2 = call(
        second_kernel,
        "second",
        [((8, BLOCK2, 128), BF16)],
        other1, part, sums, ptdf_out, own_t, screened,
    )
    got2 = lax.all_to_all(block2, "cont", 0, 0, tiled=True)
    turned, direct, worst_part = call(
        combine_kernel,
        "combine",
        [((128, 128), F32), ((128, 128), F32), ((8, 128), F32)],
        got2, got1, other1, ratings,
        scratch=[pltpu.VMEM((128, 8), F32)],
    )

    def index(c, y, core, q):
        return ((c * sizes[1] + y) * sizes[2] + core) * sizes[3] + q

    pairs = [
        (index(c, y, core, q), index(c, y ^ (core * 2 + c // 4), core, q ^ (c % 4)))
        for c in range(sizes[0])
        for y in range(sizes[1])
        for core in range(sizes[2])
        for q in range(sizes[3])
    ]
    turned = lax.ppermute(turned, EVERY, pairs)
    block3 = call(
        functools.partial(finish_kernel, scale),
        "finish",
        [((16, BLOCK3, 128), I16)],
        turned, direct, worst_part,
    )
    got3 = lax.all_to_all(block3, ("cont", "core"), 0, 0, tiled=True)
    schur, worst_t = call(
        place_kernel, "place", [((64, 2048), F32), ((64, 128), F32)], got3
    )
    return worst_t.T, schur


def solution(mesh):
    n_cont, n_line, n_scen = (mesh.shape[a] for a in ("cont", "line", "scen"))
    fine = Mesh(mesh.devices.reshape(n_cont, n_line // 2, 2, n_scen), EVERY)
    line = ("y", "core")
    every = P(EVERY)
    in_specs = (
        P(line, "cont"),
        P(line, "scen"),
        P("scen", "cont"),
        P(line),
        P(line, None),
        P("cont", None),
        every,
        every,
        every,
        every,
    )
    out_specs = (P(line, "scen"), P((*line, "scen"), None))
    return jax.shard_map(local, mesh=fine, in_specs=in_specs, out_specs=out_specs, check_vma=False)
```

```python
import functools

import jax
import jax.numpy as jnp
from jax import lax
from jax.experimental import pallas as pl
from jax.experimental.pallas import tpu as pltpu
from jax.sharding import Mesh
from jax.sharding import PartitionSpec as P


F32 = jnp.float32
BF16 = jnp.bfloat16
I16 = jnp.int16

M_OWN = 0
M_TILE = 32
LIST = 64
BLOCK1 = 96

TAIL2 = 128
BLOCK2 = 160

BLOCK3 = 80


def iota(shape, axis):
    return lax.broadcasted_iota(jnp.int32, shape, axis)


def dot(a, b, dims):
    return lax.dot_general(a, b, (dims, ((), ())), preferred_element_type=F32)


NN = ((1,), (0,))
NT = ((1,), (1,))
TN = ((0,), (0,))


def split(x):
    high = x.astype(BF16)
    return high, (x - high.astype(F32)).astype(BF16)


def split3(x):
    high = x.astype(BF16)
    rest = x - high.astype(F32)
    mid, low = split(rest)
    return high, mid, low


ORDER1 = (16, False, 15)
ORDER2 = (8, False, 4)
ORDER3 = (8, False, 0, True)


def spot(order, n, core):
    size, reverse, other = order[:3]
    bits = size.bit_length() - 1
    if reverse:
        n = sum(((n >> i) & 1) << (bits - 1 - i) for i in range(bits))
    return n ^ (other * core) if other else n


def spot3(c, core):
    at = spot(ORDER3, c, core)
    return core * 8 + at if ORDER3[3] else at * 2 + core


def listed(order):
    names = [sorted(range(order[0]), key=lambda n: spot(order, n, core)) for core in range(2)]
    return names


def place():
    return tuple(lax.axis_index(a) for a in ("cont", "y", "core", "scen"))


def prep_kernel(*refs):
    hbm, out, local, sems = refs[:9], refs[9], refs[10:19], refs[19]
    c, y, core, q = place()
    lines_here = pl.ds(pl.multiple_of(q * 32, 32), 32)
    copies = []
    for i, (source, target) in enumerate(zip(hbm, local)):
        source = source.at[lines_here, :] if i == 8 else source
        copies.append(pltpu.make_async_copy(source, target, sems.at[i]))
    for copy in copies:
        copy.start()
    for copy in copies:
        copy.wait()
    used, k4, l4, s4, lodf, flow, out_flow, limits, own_ref = local
    n = 512

    def row(ref):
        return jnp.concatenate([ref[j : j + 1, :] for j in range(4)], axis=1)

    k, l, s = row(k4), row(l4), row(s4)
    lines, conts = lodf.shape
    scens = flow.shape[0]
    is_l = iota((lines, n), 0) == l
    is_s = iota((scens, n), 0) == s
    one_l = jnp.where(is_l, 1.0, 0.0).astype(BF16)
    one_k = jnp.where(iota((conts, n), 0) == k, 1.0, 0.0).astype(BF16)
    by_k = dot(jnp.concatenate([lodf[...], *split3(out_flow[...])], axis=0), one_k, NN)
    coef = jnp.sum(jnp.where(is_l, by_k[:lines], 0.0), axis=0, keepdims=True)
    outs = by_k[lines : lines + scens] + by_k[lines + scens : lines + 2 * scens]
    outs = outs + by_k[lines + 2 * scens :]
    outs = jnp.sum(jnp.where(is_s, outs, 0.0), axis=0, keepdims=True)
    ratings = jnp.broadcast_to(limits[...], (16, lines))
    by_l = dot(jnp.concatenate([*split3(flow[...]), *split3(ratings)], axis=0), one_l, NN)
    flows = by_l[:scens] + by_l[scens : 2 * scens] + by_l[2 * scens : 3 * scens]
    flows = jnp.sum(jnp.where(is_s, flows, 0.0), axis=0, keepdims=True)
    base = 3 * scens
    rating = by_l[base : base + 1] + by_l[base + 16 : base + 17] + by_l[base + 32 : base + 33]
    ratio = (flows + coef * outs) / rating
    weight = jnp.where(iota((1, n), 1) < used[0], 1.0 + ratio * ratio, 0.0)
    mixed = weight * coef
    square = mixed * coef

    def rows16(x):
        parts = [p.astype(F32) for p in split3(x)]
        return jnp.concatenate([*parts, jnp.zeros((13, n), F32)], axis=0).astype(BF16)

    e_parts = dot(rows16(square), one_k, NT)
    e_sum = e_parts[0:1] + e_parts[1:2] + e_parts[2:3]
    d_parts = dot(rows16(weight), one_l, NT)
    d_sum = d_parts[0:1] + d_parts[1:2] + d_parts[2:3]

    upper = k >= conts // 2
    kl = jnp.where(upper, k - conts // 2, k)
    fields = [
        l.astype(F32),
        kl.astype(F32),
        jnp.where(upper, 0.0, mixed),
        jnp.where(upper, mixed, 0.0),
        *[p.astype(F32) for p in split(e_sum)],
    ]
    rows = [f[:, 128 * j : 128 * j + 128] for f in fields for j in range(4)]
    rows += [p.astype(F32) for p in split(d_sum)]
    rows += [jnp.zeros((32 - len(rows), 128), F32)]
    table = jnp.concatenate(rows, axis=0).astype(BF16)
    for b in range(16):
        out[b, LIST : LIST + 32, :] = table

    own = own_ref[...]
    for yy in range(4):
        for qq in range(4):
            first = 512 * yy + 64 * qq
            part = jnp.concatenate(
                [own[:, first : first + 64], own[:, first + 256 : first + 320]], axis=1
            )
            out[spot(ORDER1, yy * 4 + qq, core), M_OWN : M_OWN + 32, :] = part
            for cc in range(2):
                to_y = lax.bitwise_xor(jnp.int32(yy), 2 * cc + c // 4)
                to = to_y * 4 + lax.bitwise_xor(jnp.int32(qq), c % 4)
                lines = jnp.where(to < yy * 4 + qq, part[0:16].astype(F32), part[16:32].astype(F32))
                first_row = M_TILE + 16 * cc
                out[spot(ORDER1, to, core), first_row : first_row + 16, :] = lines.astype(BF16)


def half_product(got, core):
    def at(n):
        return spot(ORDER1, n, core)

    def pieces(f, j):
        l, kl, low, up = f[j : j + 1], f[4 + j : 5 + j], f[8 + j : 9 + j], f[12 + j : 13 + j]
        is_l = iota((128, 128), 0).astype(F32) == l
        left = jnp.concatenate(
            [jnp.where(is_l, low, 0.0), jnp.where(is_l, up, 0.0)], axis=0
        ).astype(BF16)
        right = jnp.where(iota((256, 128), 0).astype(F32) == kl, 1.0, 0.0).astype(BF16)
        return left, right

    e_sum, d_rows, cores = jnp.zeros((8, 128), F32), [], []
    for yy in range(4):
        tables = [got[at(yy * 4 + r), LIST : LIST + 32, :].astype(F32) for r in range(4)]
        both = [pieces(f, j) for f in tables for j in range(4)]
        blocks = dot(
            jnp.concatenate([p[0] for p in both], axis=1),
            jnp.concatenate([p[1] for p in both], axis=1),
            NT,
        )
        cores.append(jnp.concatenate([blocks[:128], blocks[128:]], axis=1))
        total = tables[0] + tables[1] + tables[2] + tables[3]
        e_sum = e_sum + total[16:24]
        d_rows.append(total[24:25] + total[25:26])
    mon = jnp.concatenate([got[at(i), M_OWN : M_OWN + 32, :] for i in range(16)], axis=0)
    high, low = split(jnp.concatenate(cores, axis=0))
    part = dot(mon, high, TN) + dot(mon, low, TN)
    return part, jnp.concatenate([e_sum[0:4] + e_sum[4:8], *d_rows], axis=0)


def first_kernel(got, part, sums):
    part[...], sums[...] = half_product(got, lax.axis_index("core"))


def second_kernel(got, part1, sums1, out_rows, own_t, screened, sent):
    c, y, core, q = place()
    part, sums = half_product(got, 1 - core)
    e_sum = sums1[0:4, :] + sums[0:4]
    e_row = jnp.concatenate([e_sum[j : j + 1] for j in range(4)], axis=1)
    part = part1[...] + part + (0.5 * e_row) * own_t[...].astype(F32)
    left = jnp.concatenate(split(part), axis=0)
    d_all = jnp.concatenate([sums1[4:8, :], sums[4:8]], axis=0)
    d_rows = [p.astype(F32) for p in split(d_all)]
    for i in range(8):
        w_rows = [p.astype(F32) for p in split(screened[8 * i : 8 * i + 8, :])]
        sent[spot(ORDER2, i, core), TAIL2:BLOCK2, :] = jnp.concatenate([*w_rows, *d_rows], axis=0).astype(BF16)
    half = lax.bitwise_xor(y // 2, core)
    for yy in range(2):
        first = pl.multiple_of(half * 1024 + 512 * yy, 512)
        both = dot(left, out_rows[:, pl.ds(first, 512)], NN)
        tile = (both[:128] + both[128:]).astype(BF16)
        for qq in range(4):
            to = lax.bitwise_xor(jnp.int32(yy), y % 2) * 4 + lax.bitwise_xor(jnp.int32(qq), q)
            sent[spot(ORDER2, to, core), 0:128, :] = jnp.concatenate(
                [tile[:, 64 * qq : 64 * qq + 64], tile[:, 256 + 64 * qq : 320 + 64 * qq]], axis=1
            )


def combine_kernel(got2, own, other, limits, turned, direct, worst, d_ref):
    c, y, core, q = place()
    a = got2[0, 0:128, :].astype(F32)
    tail = got2[0, TAIL2:BLOCK2, :].astype(F32)
    high = tail[0:8] + tail[8:16]
    d_all = tail[16:24] + tail[24:32]
    for i in range(1, 8):
        a = a + got2[i, 0:128, :].astype(F32)
        tail = got2[i, TAIL2:BLOCK2, :].astype(F32)
        high = jnp.maximum(high, tail[0:8] + tail[8:16])
        d_all = d_all + (tail[16:24] + tail[24:32])
    worst[...] = high / limits[...]
    d_ref[...] = d_all.T

    def side(h):
        lefts = []
        for i, got in enumerate((own, other)):
            for yy in range(4):
                for r in range(4):
                    lines = pl.ds(pl.multiple_of(32 * r + 16 * h, 16), 16)
                    n = spot(ORDER1, yy * 4 + r, core if i == 0 else 1 - core)
                    mon = got[n, pl.ds(pl.multiple_of(M_OWN + 16 * h, 16), 16), :]
                    scaled = mon.astype(F32) * d_ref[lines, 4 * i + yy : 4 * i + yy + 1]
                    lefts.append(jnp.concatenate(split(scaled), axis=1))
        return jnp.concatenate(lefts, axis=0)

    def write(both, factor):
        total = a + factor * (both[:128] + both[128:])
        direct[...] = total
        turned[...] = total.T

    alone = (c == 0) & (core == 0)

    @pl.when(alone)
    def _():
        both = 0.0
        for h in range(2):
            rights = [
                g[spot(ORDER1, n, k), M_OWN + 16 * h : M_OWN + 16 * h + 16, :]
                for g, k in ((own, core), (other, 1 - core))
                for n in range(16)
            ]
            both = both + dot(side(h), jnp.concatenate(rights, axis=0), TN)
        write(both, 0.5)

    @pl.when(jnp.logical_not(alone))
    def _():
        to_y = lax.bitwise_xor(y, 2 * core + c // 4)
        to_q = lax.bitwise_xor(q, c % 4)
        h = jnp.where(y * 4 + q < to_y * 4 + to_q, 0, 1)
        there = pl.ds(pl.multiple_of(M_TILE + 16 * core, 16), 16)
        rights = [
            g[spot(ORDER1, n, k), there, :]
            for g, k in ((own, core), (other, 1 - core))
            for n in range(16)
        ]
        write(dot(side(h), jnp.concatenate(rights, axis=0), TN), 1.0)


def encode(x):
    top = jnp.maximum(jnp.max(jnp.abs(x), axis=0, keepdims=True), 1e-30)
    exponent = jnp.floor(jnp.log2(top) + 1.001) - 15.0
    return jnp.floor(x * jnp.exp2(-exponent) + 0.5), exponent


def finish_kernel(scale, turned, direct, worst, sent):
    tile = (direct[...] + turned[...]) * scale
    worst_code, worst_exp = encode(worst[...])
    for core in range(2):
        code, exp = encode(tile[64 * core : 64 * core + 64, :])
        rows = [code, worst_code, exp, worst_exp, jnp.zeros((BLOCK3 - 74, 128), F32)]
        block = jnp.concatenate(rows, axis=0).astype(jnp.int32).astype(I16)
        for i in range(8):
            sent[spot3(i, core), :, :] = block


def decode(code, exponent):
    return code * jnp.exp2(exponent)


def place_kernel(got, schur, worst):
    c, y, core, q = place()
    for yy in range(4):
        parts = []
        for qq in range(4):
            source_c = lax.bitwise_xor(jnp.int32(yy % 2), y % 2) * 4
            source_c = source_c + lax.bitwise_xor(jnp.int32(qq), q)
            source_core = lax.bitwise_xor(jnp.int32(yy // 2), y // 2)
            block = got[spot3(source_c, source_core), :, :].astype(jnp.int32).astype(F32)
            parts.append(decode(block[0:64], block[72:73]))
        schur[:, 512 * yy : 512 * yy + 512] = jnp.concatenate(
            [p[:, :64] for p in parts] + [p[:, 64:] for p in parts], axis=1
        )
    for i in range(8):
        block = got[spot3(i, core), 64:80, :].astype(jnp.int32).astype(F32)
        worst[8 * i : 8 * i + 8, :] = decode(block[0:8], block[9:10])


def call(kernel, name, outs, *args, scratch=(), space=pltpu.VMEM, vmem_mib=24):
    vmem = pl.BlockSpec(memory_space=pltpu.VMEM)
    specs = [vmem] * len(outs)
    shapes = [jax.ShapeDtypeStruct(s, d) for s, d in outs]
    many = len(outs) > 1
    return pl.pallas_call(
        kernel,
        name=name,
        out_shape=shapes if many else shapes[0],
        in_specs=[pl.BlockSpec(memory_space=space)] * len(args),
        out_specs=specs if many else specs[0],
        scratch_shapes=list(scratch),
        compiler_params=pltpu.CompilerParams(vmem_limit_bytes=vmem_mib * 1024 * 1024),
    )(*args)


EVERY = ("cont", "y", "core", "scen")


def local(
    lodf, flow, out_flow, limits, ptdf_mon, ptdf_out, viol_cont, viol_line, viol_scen, rows_used
):
    sizes = [lax.axis_size(a) for a in EVERY]
    n_rows = viol_cont.shape[0]
    scale = 1.0 / (n_rows * sizes[0] * sizes[1] * sizes[2] * sizes[3])
    ratings = limits.reshape(1, -1)
    flow_t = flow.T

    inputs = [
        rows_used,
        viol_cont.reshape(4, 128),
        viol_line.reshape(4, 128),
        viol_scen.reshape(4, 128),
        lodf,
        flow_t,
        out_flow,
        ratings,
        ptdf_mon,
    ]
    scratch = [pltpu.SMEM(rows_used.shape, jnp.int32)]
    scratch += [pltpu.VMEM(a.shape, a.dtype) for a in inputs[1:8]]
    scratch += [pltpu.VMEM((32, ptdf_mon.shape[1]), BF16), pltpu.SemaphoreType.DMA((9,))]
    block1 = call(
        prep_kernel, "prep", [((16, BLOCK1, 128), BF16)], *inputs, scratch=scratch, space=pl.ANY, vmem_mib=60
    )
    groups1 = [
        [((n // 4) * 2 + core) * 4 + n % 4 for n in names]
        for core, names in enumerate(listed(ORDER1))
    ]
    got1 = lax.all_to_all(
        block1, ("y", "core", "scen"), 0, 0, axis_index_groups=groups1, tiled=True
    )
    other1 = lax.ppermute(got1, "core", [(0, 1), (1, 0)])

    wide = lodf.astype(F32)
    terms = wide[None, :, :] * out_flow[:, None, :]
    screened = jnp.maximum(
        jnp.abs(flow_t + jnp.max(terms, axis=2)), jnp.abs(flow_t + jnp.min(terms, axis=2))
    )
    first = 512 * lax.axis_index("y") + 64 * lax.axis_index("scen")
    own_t = jnp.concatenate(
        [lax.dynamic_slice_in_dim(ptdf_out, first + 256 * i, 64, 1) for i in range(2)], axis=1
    ).T

    part, sums = call(first_kernel, "first", [((128, 512), F32), ((8, 128), F32)], got1)
    block2 = call(
        second_kernel,
        "second",
        [((8, BLOCK2, 128), BF16)],
        other1, part, sums, ptdf_out, own_t, screened,
    )
    groups2 = [[c * 2 + core for c in names] for core, names in enumerate(listed(ORDER2))]
    got2 = lax.all_to_all(
        block2, ("cont", "core"), 0, 0, axis_index_groups=groups2, tiled=True
    )
    turned, direct, worst_part = call(
        combine_kernel,
        "combine",
        [((128, 128), F32), ((128, 128), F32), ((8, 128), F32)],
        got2, got1, other1, ratings,
        scratch=[pltpu.VMEM((128, 8), F32)],
    )

    def index(c, y, core, q):
        return ((c * sizes[1] + y) * sizes[2] + core) * sizes[3] + q

    pairs = [
        (index(c, y, core, q), index(c, y ^ (core * 2 + c // 4), core, q ^ (c % 4)))
        for c in range(sizes[0])
        for y in range(sizes[1])
        for core in range(sizes[2])
        for q in range(sizes[3])
    ]
    turned = lax.ppermute(turned, EVERY, pairs)
    block3 = call(
        functools.partial(finish_kernel, scale),
        "finish",
        [((16, BLOCK3, 128), I16)],
        turned, direct, worst_part,
    )
    group3 = sorted(range(16), key=lambda n: spot3(n // 2, n % 2))
    got3 = lax.all_to_all(
        block3, ("cont", "core"), 0, 0, axis_index_groups=[group3], tiled=True
    )
    schur, worst_t = call(
        place_kernel, "place", [((64, 2048), F32), ((64, 128), F32)], got3
    )
    return worst_t.T, schur


def solution(mesh):
    n_cont, n_line, n_scen = (mesh.shape[a] for a in ("cont", "line", "scen"))
    fine = Mesh(mesh.devices.reshape(n_cont, n_line // 2, 2, n_scen), EVERY)
    line = ("y", "core")
    every = P(EVERY)
    in_specs = (
        P(line, "cont"),
        P(line, "scen"),
        P("scen", "cont"),
        P(line),
        P(line, None),
        P("cont", None),
        every,
        every,
        every,
        every,
    )
    out_specs = (P(line, "scen"), P((*line, "scen"), None))
    return jax.shard_map(local, mesh=fine, in_specs=in_specs, out_specs=out_specs, check_vma=False)
```

```python
import functools

import jax
import jax.numpy as jnp
from jax import lax
from jax.experimental import pallas as pl
from jax.experimental.pallas import tpu as pltpu
from jax.sharding import Mesh
from jax.sharding import PartitionSpec as P


F32 = jnp.float32
BF16 = jnp.bfloat16
I16 = jnp.int16

M_OWN = 0
M_TILE = 32
LIST = 64
BLOCK1 = 96

TAIL2 = 128
BLOCK2 = 160

BLOCK3 = 80


def iota(shape, axis):
    return lax.broadcasted_iota(jnp.int32, shape, axis)


def dot(a, b, dims):
    return lax.dot_general(a, b, (dims, ((), ())), preferred_element_type=F32)


NN = ((1,), (0,))
NT = ((1,), (1,))
TN = ((0,), (0,))


def split(x):
    high = x.astype(BF16)
    return high, (x - high.astype(F32)).astype(BF16)


def split3(x):
    high = x.astype(BF16)
    rest = x - high.astype(F32)
    mid, low = split(rest)
    return high, mid, low


ORDER1 = (16, False, 15)
ORDER2 = (8, False, 4)
ORDER3 = (8, False, 0, True)


def spot(order, n, core):
    size, reverse, other = order[:3]
    bits = size.bit_length() - 1
    if reverse:
        n = sum(((n >> i) & 1) << (bits - 1 - i) for i in range(bits))
    return n ^ (other * core) if other else n


def spot3(c, core):
    at = spot(ORDER3, c, core)
    return core * 8 + at if ORDER3[3] else at * 2 + core


def listed(order):
    names = [sorted(range(order[0]), key=lambda n: spot(order, n, core)) for core in range(2)]
    return names


def place():
    return tuple(lax.axis_index(a) for a in ("cont", "y", "core", "scen"))


def prep_kernel(*refs):
    hbm, out, local, sems = refs[:9], refs[9], refs[10:19], refs[19]
    c, y, core, q = place()
    lines_here = pl.ds(pl.multiple_of(q * 32, 32), 32)
    copies = []
    for i, (source, target) in enumerate(zip(hbm, local)):
        source = source.at[lines_here, :] if i == 8 else source
        copies.append(pltpu.make_async_copy(source, target, sems.at[i]))
    for copy in copies:
        copy.start()
    for copy in copies:
        copy.wait()
    used, k4, l4, s4, lodf, flow, out_flow, limits, own_ref = local
    n = 512

    def row(ref):
        return jnp.concatenate([ref[j : j + 1, :] for j in range(4)], axis=1)

    k, l, s = row(k4), row(l4), row(s4)
    lines, conts = lodf.shape
    scens = flow.shape[0]
    is_l = iota((lines, n), 0) == l
    is_s = iota((scens, n), 0) == s
    one_l = jnp.where(is_l, 1.0, 0.0).astype(BF16)
    one_k = jnp.where(iota((conts, n), 0) == k, 1.0, 0.0).astype(BF16)
    by_k = dot(jnp.concatenate([lodf[...], *split3(out_flow[...])], axis=0), one_k, NN)
    coef = jnp.sum(jnp.where(is_l, by_k[:lines], 0.0), axis=0, keepdims=True)
    outs = by_k[lines : lines + scens] + by_k[lines + scens : lines + 2 * scens]
    outs = outs + by_k[lines + 2 * scens :]
    outs = jnp.sum(jnp.where(is_s, outs, 0.0), axis=0, keepdims=True)
    ratings = jnp.broadcast_to(limits[...], (16, lines))
    by_l = dot(jnp.concatenate([*split3(flow[...]), *split3(ratings)], axis=0), one_l, NN)
    flows = by_l[:scens] + by_l[scens : 2 * scens] + by_l[2 * scens : 3 * scens]
    flows = jnp.sum(jnp.where(is_s, flows, 0.0), axis=0, keepdims=True)
    base = 3 * scens
    rating = by_l[base : base + 1] + by_l[base + 16 : base + 17] + by_l[base + 32 : base + 33]
    ratio = (flows + coef * outs) / rating
    weight = jnp.where(iota((1, n), 1) < used[0], 1.0 + ratio * ratio, 0.0)
    mixed = weight * coef
    square = mixed * coef

    def rows16(x):
        parts = [p.astype(F32) for p in split3(x)]
        return jnp.concatenate([*parts, jnp.zeros((13, n), F32)], axis=0).astype(BF16)

    e_parts = dot(rows16(square), one_k, NT)
    e_sum = e_parts[0:1] + e_parts[1:2] + e_parts[2:3]
    d_parts = dot(rows16(weight), one_l, NT)
    d_sum = d_parts[0:1] + d_parts[1:2] + d_parts[2:3]

    upper = k >= conts // 2
    kl = jnp.where(upper, k - conts // 2, k)
    fields = [
        l.astype(F32),
        kl.astype(F32),
        jnp.where(upper, 0.0, mixed),
        jnp.where(upper, mixed, 0.0),
        *[p.astype(F32) for p in split(e_sum)],
    ]
    rows = [f[:, 128 * j : 128 * j + 128] for f in fields for j in range(4)]
    rows += [p.astype(F32) for p in split(d_sum)]
    rows += [jnp.zeros((32 - len(rows), 128), F32)]
    table = jnp.concatenate(rows, axis=0).astype(BF16)
    for b in range(16):
        out[b, LIST : LIST + 32, :] = table

    own = own_ref[...]
    for yy in range(4):
        for qq in range(4):
            first = 512 * yy + 64 * qq
            part = jnp.concatenate(
                [own[:, first : first + 64], own[:, first + 256 : first + 320]], axis=1
            )
            out[spot(ORDER1, yy * 4 + qq, core), M_OWN : M_OWN + 32, :] = part
            for cc in range(2):
                to_y = lax.bitwise_xor(jnp.int32(yy), 2 * cc + c // 4)
                to = to_y * 4 + lax.bitwise_xor(jnp.int32(qq), c % 4)
                lines = jnp.where(to < yy * 4 + qq, part[0:16].astype(F32), part[16:32].astype(F32))
                first_row = M_TILE + 16 * cc
                out[spot(ORDER1, to, core), first_row : first_row + 16, :] = lines.astype(BF16)


def half_product(got, core):
    def at(n):
        return spot(ORDER1, n, core)

    def pieces(f, j):
        l, kl, low, up = f[j : j + 1], f[4 + j : 5 + j], f[8 + j : 9 + j], f[12 + j : 13 + j]
        is_l = iota((128, 128), 0).astype(F32) == l
        left = jnp.concatenate(
            [jnp.where(is_l, low, 0.0), jnp.where(is_l, up, 0.0)], axis=0
        ).astype(BF16)
        right = jnp.where(iota((256, 128), 0).astype(F32) == kl, 1.0, 0.0).astype(BF16)
        return left, right

    e_sum, d_rows, cores = jnp.zeros((8, 128), F32), [], []
    for yy in range(4):
        tables = [got[at(yy * 4 + r), LIST : LIST + 32, :].astype(F32) for r in range(4)]
        both = [pieces(f, j) for f in tables for j in range(4)]
        blocks = dot(
            jnp.concatenate([p[0] for p in both], axis=1),
            jnp.concatenate([p[1] for p in both], axis=1),
            NT,
        )
        cores.append(jnp.concatenate([blocks[:128], blocks[128:]], axis=1))
        total = tables[0] + tables[1] + tables[2] + tables[3]
        e_sum = e_sum + total[16:24]
        d_rows.append(total[24:25] + total[25:26])
    mon = jnp.concatenate([got[at(i), M_OWN : M_OWN + 32, :] for i in range(16)], axis=0)
    high, low = split(jnp.concatenate(cores, axis=0))
    part = dot(mon, high, TN) + dot(mon, low, TN)
    return part, jnp.concatenate([e_sum[0:4] + e_sum[4:8], *d_rows], axis=0)


def first_kernel(got, part, sums):
    part[...], sums[...] = half_product(got, lax.axis_index("core"))


def second_kernel(got, part1, sums1, out_rows, own_t, screened, sent):
    c, y, core, q = place()
    part, sums = half_product(got, 1 - core)
    e_sum = sums1[0:4, :] + sums[0:4]
    e_row = jnp.concatenate([e_sum[j : j + 1] for j in range(4)], axis=1)
    part = part1[...] + part + (0.5 * e_row) * own_t[...].astype(F32)
    left = jnp.concatenate(split(part), axis=0)
    d_all = jnp.concatenate([sums1[4:8, :], sums[4:8]], axis=0)
    d_rows = [p.astype(F32) for p in split(d_all)]
    for i in range(8):
        w_rows = [p.astype(F32) for p in split(screened[8 * i : 8 * i + 8, :])]
        sent[spot(ORDER2, i, core), TAIL2:BLOCK2, :] = jnp.concatenate([*w_rows, *d_rows], axis=0).astype(BF16)
    half = lax.bitwise_xor(y // 2, core)
    for yy in range(2):
        first = pl.multiple_of(half * 1024 + 512 * yy, 512)
        both = dot(left, out_rows[:, pl.ds(first, 512)], NN)
        tile = (both[:128] + both[128:]).astype(BF16)
        for qq in range(4):
            to = lax.bitwise_xor(jnp.int32(yy), y % 2) * 4 + lax.bitwise_xor(jnp.int32(qq), q)
            sent[spot(ORDER2, to, core), 0:128, :] = jnp.concatenate(
                [tile[:, 64 * qq : 64 * qq + 64], tile[:, 256 + 64 * qq : 320 + 64 * qq]], axis=1
            )


def encode(x):
    top = jnp.maximum(jnp.max(jnp.abs(x), axis=0, keepdims=True), 1e-30)
    exponent = jnp.floor(jnp.log2(top) + 1.001) - 15.0
    return jnp.floor(x * jnp.exp2(-exponent) + 0.5), exponent


def decode(code, exponent):
    return code * jnp.exp2(exponent)


def combine_kernel(got2, own, other, limits, turned, direct, worst, d_ref):
    c, y, core, q = place()
    a = got2[0, 0:128, :].astype(F32)
    tail = got2[0, TAIL2:BLOCK2, :].astype(F32)
    high = tail[0:8] + tail[8:16]
    d_all = tail[16:24] + tail[24:32]
    for i in range(1, 8):
        a = a + got2[i, 0:128, :].astype(F32)
        tail = got2[i, TAIL2:BLOCK2, :].astype(F32)
        high = jnp.maximum(high, tail[0:8] + tail[8:16])
        d_all = d_all + (tail[16:24] + tail[24:32])
    worst[...] = high / limits[...]
    d_ref[...] = d_all.T

    def side(h):
        lefts = []
        for i, got in enumerate((own, other)):
            for yy in range(4):
                for r in range(4):
                    lines = pl.ds(pl.multiple_of(32 * r + 16 * h, 16), 16)
                    n = spot(ORDER1, yy * 4 + r, core if i == 0 else 1 - core)
                    mon = got[n, pl.ds(pl.multiple_of(M_OWN + 16 * h, 16), 16), :]
                    scaled = mon.astype(F32) * d_ref[lines, 4 * i + yy : 4 * i + yy + 1]
                    lefts.append(jnp.concatenate(split(scaled), axis=1))
        return jnp.concatenate(lefts, axis=0)

    def write(both, factor):
        total = a + factor * (both[:128] + both[128:])
        direct[...] = total
        code, exp = encode(total.T)
        rows = [code, exp, jnp.zeros((15, 128), F32)]
        turned[...] = jnp.concatenate(rows, axis=0).astype(jnp.int32).astype(I16)

    alone = (c == 0) & (core == 0)

    @pl.when(alone)
    def _():
        both = 0.0
        for h in range(2):
            rights = [
                g[spot(ORDER1, n, k), M_OWN + 16 * h : M_OWN + 16 * h + 16, :]
                for g, k in ((own, core), (other, 1 - core))
                for n in range(16)
            ]
            both = both + dot(side(h), jnp.concatenate(rights, axis=0), TN)
        write(both, 0.5)

    @pl.when(jnp.logical_not(alone))
    def _():
        to_y = lax.bitwise_xor(y, 2 * core + c // 4)
        to_q = lax.bitwise_xor(q, c % 4)
        h = jnp.where(y * 4 + q < to_y * 4 + to_q, 0, 1)
        there = pl.ds(pl.multiple_of(M_TILE + 16 * core, 16), 16)
        rights = [
            g[spot(ORDER1, n, k), there, :]
            for g, k in ((own, core), (other, 1 - core))
            for n in range(16)
        ]
        write(dot(side(h), jnp.concatenate(rights, axis=0), TN), 1.0)


def finish_kernel(scale, turned, direct, worst, sent):
    other = turned[...].astype(jnp.int32).astype(F32)
    tile = (direct[...] + decode(other[:128], other[128:129])) * scale
    worst_code, worst_exp = encode(worst[...])
    for core in range(2):
        code, exp = encode(tile[64 * core : 64 * core + 64, :])
        rows = [code, worst_code, exp, worst_exp, jnp.zeros((BLOCK3 - 74, 128), F32)]
        block = jnp.concatenate(rows, axis=0).astype(jnp.int32).astype(I16)
        for i in range(8):
            sent[spot3(i, core), :, :] = block


def place_kernel(got, schur, worst):
    c, y, core, q = place()
    for yy in range(4):
        parts = []
        for qq in range(4):
            source_c = lax.bitwise_xor(jnp.int32(yy % 2), y % 2) * 4
            source_c = source_c + lax.bitwise_xor(jnp.int32(qq), q)
            source_core = lax.bitwise_xor(jnp.int32(yy // 2), y // 2)
            block = got[spot3(source_c, source_core), :, :].astype(jnp.int32).astype(F32)
            parts.append(decode(block[0:64], block[72:73]))
        schur[:, 512 * yy : 512 * yy + 512] = jnp.concatenate(
            [p[:, :64] for p in parts] + [p[:, 64:] for p in parts], axis=1
        )
    for i in range(8):
        block = got[spot3(i, core), 64:80, :].astype(jnp.int32).astype(F32)
        worst[8 * i : 8 * i + 8, :] = decode(block[0:8], block[9:10])


def call(kernel, name, outs, *args, scratch=(), space=pltpu.VMEM, vmem_mib=24):
    vmem = pl.BlockSpec(memory_space=pltpu.VMEM)
    specs = [vmem] * len(outs)
    shapes = [jax.ShapeDtypeStruct(s, d) for s, d in outs]
    many = len(outs) > 1
    return pl.pallas_call(
        kernel,
        name=name,
        out_shape=shapes if many else shapes[0],
        in_specs=[pl.BlockSpec(memory_space=space)] * len(args),
        out_specs=specs if many else specs[0],
        scratch_shapes=list(scratch),
        compiler_params=pltpu.CompilerParams(vmem_limit_bytes=vmem_mib * 1024 * 1024),
    )(*args)


EVERY = ("cont", "y", "core", "scen")


def local(
    lodf, flow, out_flow, limits, ptdf_mon, ptdf_out, viol_cont, viol_line, viol_scen, rows_used
):
    sizes = [lax.axis_size(a) for a in EVERY]
    n_rows = viol_cont.shape[0]
    scale = 1.0 / (n_rows * sizes[0] * sizes[1] * sizes[2] * sizes[3])
    ratings = limits.reshape(1, -1)
    flow_t = flow.T

    inputs = [
        rows_used,
        viol_cont.reshape(4, 128),
        viol_line.reshape(4, 128),
        viol_scen.reshape(4, 128),
        lodf,
        flow_t,
        out_flow,
        ratings,
        ptdf_mon,
    ]
    scratch = [pltpu.SMEM(rows_used.shape, jnp.int32)]
    scratch += [pltpu.VMEM(a.shape, a.dtype) for a in inputs[1:8]]
    scratch += [pltpu.VMEM((32, ptdf_mon.shape[1]), BF16), pltpu.SemaphoreType.DMA((9,))]
    block1 = call(
        prep_kernel, "prep", [((16, BLOCK1, 128), BF16)], *inputs, scratch=scratch, space=pl.ANY, vmem_mib=60
    )
    groups1 = [
        [((n // 4) * 2 + core) * 4 + n % 4 for n in names]
        for core, names in enumerate(listed(ORDER1))
    ]
    got1 = lax.all_to_all(
        block1, ("y", "core", "scen"), 0, 0, axis_index_groups=groups1, tiled=True
    )

    wide = lodf.astype(F32)
    terms = wide[None, :, :] * out_flow[:, None, :]
    screened = jnp.maximum(
        jnp.abs(flow_t + jnp.max(terms, axis=2)), jnp.abs(flow_t + jnp.min(terms, axis=2))
    )
    first = 512 * lax.axis_index("y") + 64 * lax.axis_index("scen")
    own_t = jnp.concatenate(
        [lax.dynamic_slice_in_dim(ptdf_out, first + 256 * i, 64, 1) for i in range(2)], axis=1
    ).T

    got1, own_t, screened = lax.optimization_barrier((got1, own_t, screened))
    other1 = lax.ppermute(got1, "core", [(0, 1), (1, 0)])
    part, sums = call(first_kernel, "first", [((128, 512), F32), ((8, 128), F32)], got1)
    block2 = call(
        second_kernel,
        "second",
        [((8, BLOCK2, 128), BF16)],
        other1, part, sums, ptdf_out, own_t, screened,
    )
    groups2 = [[c * 2 + core for c in names] for core, names in enumerate(listed(ORDER2))]
    got2 = lax.all_to_all(
        block2, ("cont", "core"), 0, 0, axis_index_groups=groups2, tiled=True
    )
    turned, direct, worst_part = call(
        combine_kernel,
        "combine",
        [((144, 128), I16), ((128, 128), F32), ((8, 128), F32)],
        got2, got1, other1, ratings,
        scratch=[pltpu.VMEM((128, 8), F32)],
    )

    def index(c, y, core, q):
        return ((c * sizes[1] + y) * sizes[2] + core) * sizes[3] + q

    pairs = [
        (index(c, y, core, q), index(c, y ^ (core * 2 + c // 4), core, q ^ (c % 4)))
        for c in range(sizes[0])
        for y in range(sizes[1])
        for core in range(sizes[2])
        for q in range(sizes[3])
    ]
    turned = lax.ppermute(turned, EVERY, pairs)
    block3 = call(
        functools.partial(finish_kernel, scale),
        "finish",
        [((16, BLOCK3, 128), I16)],
        turned, direct, worst_part,
    )
    group3 = sorted(range(16), key=lambda n: spot3(n // 2, n % 2))
    got3 = lax.all_to_all(
        block3, ("cont", "core"), 0, 0, axis_index_groups=[group3], tiled=True
    )
    schur, worst_t = call(
        place_kernel, "place", [((64, 2048), F32), ((64, 128), F32)], got3
    )
    return worst_t.T, schur


def solution(mesh):
    n_cont, n_line, n_scen = (mesh.shape[a] for a in ("cont", "line", "scen"))
    fine = Mesh(mesh.devices.reshape(n_cont, n_line // 2, 2, n_scen), EVERY)
    line = ("y", "core")
    every = P(EVERY)
    in_specs = (
        P(line, "cont"),
        P(line, "scen"),
        P("scen", "cont"),
        P(line),
        P(line, None),
        P("cont", None),
        every,
        every,
        every,
        every,
    )
    out_specs = (P(line, "scen"), P((*line, "scen"), None))
    return jax.shard_map(local, mesh=fine, in_specs=in_specs, out_specs=out_specs, check_vma=False)
```

```python
import functools

import jax
import jax.numpy as jnp
from jax import lax
from jax.experimental import pallas as pl
from jax.experimental.pallas import tpu as pltpu
from jax.sharding import Mesh
from jax.sharding import PartitionSpec as P


F32 = jnp.float32
BF16 = jnp.bfloat16
I16 = jnp.int16

M_OWN = 0
M_TILE = 32
LIST = 64
BLOCK1 = 96

TAIL2 = 128
BLOCK2 = 160

BLOCK3 = 80


def iota(shape, axis):
    return lax.broadcasted_iota(jnp.int32, shape, axis)


def dot(a, b, dims):
    return lax.dot_general(a, b, (dims, ((), ())), preferred_element_type=F32)


NN = ((1,), (0,))
NT = ((1,), (1,))
TN = ((0,), (0,))


def split(x):
    high = x.astype(BF16)
    return high, (x - high.astype(F32)).astype(BF16)


def split3(x):
    high = x.astype(BF16)
    rest = x - high.astype(F32)
    mid, low = split(rest)
    return high, mid, low


ORDER1 = (16, False, 15)
ORDER2 = (8, False, 4)
ORDER3 = (8, False, 0, True)


def spot(order, n, core):
    size, reverse, other = order[:3]
    bits = size.bit_length() - 1
    if reverse:
        n = sum(((n >> i) & 1) << (bits - 1 - i) for i in range(bits))
    return n ^ (other * core) if other else n


def spot3(c, core):
    at = spot(ORDER3, c, core)
    return core * 8 + at if ORDER3[3] else at * 2 + core


def listed(order):
    names = [sorted(range(order[0]), key=lambda n: spot(order, n, core)) for core in range(2)]
    return names


def place():
    return tuple(lax.axis_index(a) for a in ("cont", "y", "core", "scen"))


def prep_kernel(*refs):
    hbm, out, local, sems = refs[:9], refs[9], refs[10:19], refs[19]
    block, out_sems = refs[20], refs[21]
    c, y, core, q = place()
    lines_here = pl.ds(pl.multiple_of(q * 32, 32), 32)
    copies = []
    for i, (source, target) in enumerate(zip(hbm, local)):
        source = source.at[lines_here, :] if i == 8 else source
        copies.append(pltpu.make_async_copy(source, target, sems.at[i]))
    for copy in copies[8:] + copies[:8]:
        copy.start()
    used, k4, l4, s4, lodf, flow, out_flow, limits, own_ref = local
    copies[8].wait()
    own = own_ref[...]
    for yy in range(4):
        for qq in range(4):
            first = 512 * yy + 64 * qq
            part = jnp.concatenate(
                [own[:, first : first + 64], own[:, first + 256 : first + 320]], axis=1
            )
            block[spot(ORDER1, yy * 4 + qq, core), M_OWN : M_OWN + 32, :] = part
            for cc in range(2):
                to_y = lax.bitwise_xor(jnp.int32(yy), 2 * cc + c // 4)
                to = to_y * 4 + lax.bitwise_xor(jnp.int32(qq), c % 4)
                lines = jnp.where(to < yy * 4 + qq, part[0:16].astype(F32), part[16:32].astype(F32))
                first_row = M_TILE + 16 * cc
                block[spot(ORDER1, to, core), first_row : first_row + 16, :] = lines.astype(BF16)
    mon_out = pltpu.make_async_copy(
        block.at[:, 0:LIST, :], out.at[:, 0:LIST, :], out_sems.at[0]
    )
    mon_out.start()
    for copy in copies[:8]:
        copy.wait()
    n = 512

    def row(ref):
        return jnp.concatenate([ref[j : j + 1, :] for j in range(4)], axis=1)

    k, l, s = row(k4), row(l4), row(s4)
    lines, conts = lodf.shape
    scens = flow.shape[0]
    is_l = iota((lines, n), 0) == l
    is_s = iota((scens, n), 0) == s
    one_l = jnp.where(is_l, 1.0, 0.0).astype(BF16)
    one_k = jnp.where(iota((conts, n), 0) == k, 1.0, 0.0).astype(BF16)
    by_k = dot(jnp.concatenate([lodf[...], *split3(out_flow[...])], axis=0), one_k, NN)
    coef = jnp.sum(jnp.where(is_l, by_k[:lines], 0.0), axis=0, keepdims=True)
    outs = by_k[lines : lines + scens] + by_k[lines + scens : lines + 2 * scens]
    outs = outs + by_k[lines + 2 * scens :]
    outs = jnp.sum(jnp.where(is_s, outs, 0.0), axis=0, keepdims=True)
    ratings = jnp.broadcast_to(limits[...], (16, lines))
    by_l = dot(jnp.concatenate([*split3(flow[...]), *split3(ratings)], axis=0), one_l, NN)
    flows = by_l[:scens] + by_l[scens : 2 * scens] + by_l[2 * scens : 3 * scens]
    flows = jnp.sum(jnp.where(is_s, flows, 0.0), axis=0, keepdims=True)
    base = 3 * scens
    rating = by_l[base : base + 1] + by_l[base + 16 : base + 17] + by_l[base + 32 : base + 33]
    ratio = (flows + coef * outs) / rating
    weight = jnp.where(iota((1, n), 1) < used[0], 1.0 + ratio * ratio, 0.0)
    mixed = weight * coef
    square = mixed * coef

    def rows16(x):
        parts = [p.astype(F32) for p in split3(x)]
        return jnp.concatenate([*parts, jnp.zeros((13, n), F32)], axis=0).astype(BF16)

    e_parts = dot(rows16(square), one_k, NT)
    e_sum = e_parts[0:1] + e_parts[1:2] + e_parts[2:3]
    d_parts = dot(rows16(weight), one_l, NT)
    d_sum = d_parts[0:1] + d_parts[1:2] + d_parts[2:3]

    upper = k >= conts // 2
    kl = jnp.where(upper, k - conts // 2, k)
    fields = [
        l.astype(F32),
        kl.astype(F32),
        jnp.where(upper, 0.0, mixed),
        jnp.where(upper, mixed, 0.0),
        *[p.astype(F32) for p in split(e_sum)],
    ]
    rows = [f[:, 128 * j : 128 * j + 128] for f in fields for j in range(4)]
    rows += [p.astype(F32) for p in split(d_sum)]
    rows += [jnp.zeros((32 - len(rows), 128), F32)]
    table = jnp.concatenate(rows, axis=0).astype(BF16)
    for b in range(16):
        block[b, LIST : LIST + 32, :] = table
    lists_out = pltpu.make_async_copy(
        block.at[:, LIST:BLOCK1, :], out.at[:, LIST:BLOCK1, :], out_sems.at[1]
    )
    lists_out.start()
    mon_out.wait()
    lists_out.wait()


def half_product(got, core):
    def at(n):
        return spot(ORDER1, n, core)

    def pieces(f, j):
        l, kl, low, up = f[j : j + 1], f[4 + j : 5 + j], f[8 + j : 9 + j], f[12 + j : 13 + j]
        is_l = iota((128, 128), 0).astype(F32) == l
        left = jnp.concatenate(
            [jnp.where(is_l, low, 0.0), jnp.where(is_l, up, 0.0)], axis=0
        ).astype(BF16)
        right = jnp.where(iota((256, 128), 0).astype(F32) == kl, 1.0, 0.0).astype(BF16)
        return left, right

    e_sum, d_rows, cores = jnp.zeros((8, 128), F32), [], []
    for yy in range(4):
        tables = [got[at(yy * 4 + r), LIST : LIST + 32, :].astype(F32) for r in range(4)]
        both = [pieces(f, j) for f in tables for j in range(4)]
        blocks = dot(
            jnp.concatenate([p[0] for p in both], axis=1),
            jnp.concatenate([p[1] for p in both], axis=1),
            NT,
        )
        cores.append(jnp.concatenate([blocks[:128], blocks[128:]], axis=1))
        total = tables[0] + tables[1] + tables[2] + tables[3]
        e_sum = e_sum + total[16:24]
        d_rows.append(total[24:25] + total[25:26])
    mon = jnp.concatenate([got[at(i), M_OWN : M_OWN + 32, :] for i in range(16)], axis=0)
    high, low = split(jnp.concatenate(cores, axis=0))
    part = dot(mon, high, TN) + dot(mon, low, TN)
    return part, jnp.concatenate([e_sum[0:4] + e_sum[4:8], *d_rows], axis=0)


def first_kernel(got, part, sums):
    part[...], sums[...] = half_product(got, lax.axis_index("core"))


def second_kernel(got, part1, sums1, out_rows, own_t, screened, sent):
    c, y, core, q = place()
    part, sums = half_product(got, 1 - core)
    e_sum = sums1[0:4, :] + sums[0:4]
    e_row = jnp.concatenate([e_sum[j : j + 1] for j in range(4)], axis=1)
    part = part1[...] + part + (0.5 * e_row) * own_t[...].astype(F32)
    left = jnp.concatenate(split(part), axis=0)
    d_all = jnp.concatenate([sums1[4:8, :], sums[4:8]], axis=0)
    d_rows = [p.astype(F32) for p in split(d_all)]
    for i in range(8):
        w_rows = [p.astype(F32) for p in split(screened[8 * i : 8 * i + 8, :])]
        sent[spot(ORDER2, i, core), TAIL2:BLOCK2, :] = jnp.concatenate([*w_rows, *d_rows], axis=0).astype(BF16)
    half = lax.bitwise_xor(y // 2, core)
    for yy in range(2):
        first = pl.multiple_of(half * 1024 + 512 * yy, 512)
        both = dot(left, out_rows[:, pl.ds(first, 512)], NN)
        tile = (both[:128] + both[128:]).astype(BF16)
        for qq in range(4):
            to = lax.bitwise_xor(jnp.int32(yy), y % 2) * 4 + lax.bitwise_xor(jnp.int32(qq), q)
            sent[spot(ORDER2, to, core), 0:128, :] = jnp.concatenate(
                [tile[:, 64 * qq : 64 * qq + 64], tile[:, 256 + 64 * qq : 320 + 64 * qq]], axis=1
            )


def encode(x):
    top = jnp.maximum(jnp.max(jnp.abs(x), axis=0, keepdims=True), 1e-30)
    exponent = jnp.floor(jnp.log2(top) + 1.001) - 15.0
    return jnp.floor(x * jnp.exp2(-exponent) + 0.5), exponent


def decode(code, exponent):
    return code * jnp.exp2(exponent)


def combine_kernel(got2, own, other, limits, turned, direct, worst, d_ref):
    c, y, core, q = place()
    a = got2[0, 0:128, :].astype(F32)
    tail = got2[0, TAIL2:BLOCK2, :].astype(F32)
    high = tail[0:8] + tail[8:16]
    d_all = tail[16:24] + tail[24:32]
    for i in range(1, 8):
        a = a + got2[i, 0:128, :].astype(F32)
        tail = got2[i, TAIL2:BLOCK2, :].astype(F32)
        high = jnp.maximum(high, tail[0:8] + tail[8:16])
        d_all = d_all + (tail[16:24] + tail[24:32])
    worst[...] = high / limits[...]
    d_ref[...] = d_all.T

    def side(h):
        lefts = []
        for i, got in enumerate((own, other)):
            for yy in range(4):
                for r in range(4):
                    lines = pl.ds(pl.multiple_of(32 * r + 16 * h, 16), 16)
                    n = spot(ORDER1, yy * 4 + r, core if i == 0 else 1 - core)
                    mon = got[n, pl.ds(pl.multiple_of(M_OWN + 16 * h, 16), 16), :]
                    scaled = mon.astype(F32) * d_ref[lines, 4 * i + yy : 4 * i + yy + 1]
                    lefts.append(jnp.concatenate(split(scaled), axis=1))
        return jnp.concatenate(lefts, axis=0)

    def write(both, factor):
        total = a + factor * (both[:128] + both[128:])
        direct[...] = total
        code, exp = encode(total.T)
        rows = [code, exp, jnp.zeros((15, 128), F32)]
        turned[...] = jnp.concatenate(rows, axis=0).astype(jnp.int32).astype(I16)

    alone = (c == 0) & (core == 0)

    @pl.when(alone)
    def _():
        both = 0.0
        for h in range(2):
            rights = [
                g[spot(ORDER1, n, k), M_OWN + 16 * h : M_OWN + 16 * h + 16, :]
                for g, k in ((own, core), (other, 1 - core))
                for n in range(16)
            ]
            both = both + dot(side(h), jnp.concatenate(rights, axis=0), TN)
        write(both, 0.5)

    @pl.when(jnp.logical_not(alone))
    def _():
        to_y = lax.bitwise_xor(y, 2 * core + c // 4)
        to_q = lax.bitwise_xor(q, c % 4)
        h = jnp.where(y * 4 + q < to_y * 4 + to_q, 0, 1)
        there = pl.ds(pl.multiple_of(M_TILE + 16 * core, 16), 16)
        rights = [
            g[spot(ORDER1, n, k), there, :]
            for g, k in ((own, core), (other, 1 - core))
            for n in range(16)
        ]
        write(dot(side(h), jnp.concatenate(rights, axis=0), TN), 1.0)


def finish_kernel(scale, turned, direct, worst, sent):
    other = turned[...].astype(jnp.int32).astype(F32)
    tile = (direct[...] + decode(other[:128], other[128:129])) * scale
    worst_code, worst_exp = encode(worst[...])
    for core in range(2):
        code, exp = encode(tile[64 * core : 64 * core + 64, :])
        rows = [code, worst_code, exp, worst_exp, jnp.zeros((BLOCK3 - 74, 128), F32)]
        block = jnp.concatenate(rows, axis=0).astype(jnp.int32).astype(I16)
        for i in range(8):
            sent[spot3(i, core), :, :] = block


def place_kernel(got, schur, worst):
    c, y, core, q = place()
    for yy in range(4):
        parts = []
        for qq in range(4):
            source_c = lax.bitwise_xor(jnp.int32(yy % 2), y % 2) * 4
            source_c = source_c + lax.bitwise_xor(jnp.int32(qq), q)
            source_core = lax.bitwise_xor(jnp.int32(yy // 2), y // 2)
            block = got[spot3(source_c, source_core), :, :].astype(jnp.int32).astype(F32)
            parts.append(decode(block[0:64], block[72:73]))
        schur[:, 512 * yy : 512 * yy + 512] = jnp.concatenate(
            [p[:, :64] for p in parts] + [p[:, 64:] for p in parts], axis=1
        )
    for i in range(8):
        block = got[spot3(i, core), 64:80, :].astype(jnp.int32).astype(F32)
        worst[8 * i : 8 * i + 8, :] = decode(block[0:8], block[9:10])


def call(kernel, name, outs, *args, scratch=(), space=pltpu.VMEM, first=pltpu.VMEM, vmem_mib=24):
    vmem = pl.BlockSpec(memory_space=pltpu.VMEM)
    specs = [pl.BlockSpec(memory_space=first)] + [vmem] * (len(outs) - 1)
    shapes = [jax.ShapeDtypeStruct(s, d) for s, d in outs]
    many = len(outs) > 1
    return pl.pallas_call(
        kernel,
        name=name,
        out_shape=shapes if many else shapes[0],
        in_specs=[pl.BlockSpec(memory_space=space)] * len(args),
        out_specs=specs if many else specs[0],
        scratch_shapes=list(scratch),
        compiler_params=pltpu.CompilerParams(vmem_limit_bytes=vmem_mib * 1024 * 1024),
    )(*args)


EVERY = ("cont", "y", "core", "scen")


def local(
    lodf, flow, out_flow, limits, ptdf_mon, ptdf_out, viol_cont, viol_line, viol_scen, rows_used
):
    sizes = [lax.axis_size(a) for a in EVERY]
    n_rows = viol_cont.shape[0]
    scale = 1.0 / (n_rows * sizes[0] * sizes[1] * sizes[2] * sizes[3])
    ratings = limits.reshape(1, -1)
    flow_t = flow.T

    inputs = [
        rows_used,
        viol_cont.reshape(4, 128),
        viol_line.reshape(4, 128),
        viol_scen.reshape(4, 128),
        lodf,
        flow_t,
        out_flow,
        ratings,
        ptdf_mon,
    ]
    scratch = [pltpu.SMEM(rows_used.shape, jnp.int32)]
    scratch += [pltpu.VMEM(a.shape, a.dtype) for a in inputs[1:8]]
    scratch += [pltpu.VMEM((32, ptdf_mon.shape[1]), BF16), pltpu.SemaphoreType.DMA((9,))]
    scratch += [pltpu.VMEM((16, BLOCK1, 128), BF16), pltpu.SemaphoreType.DMA((2,))]
    block1 = call(
        prep_kernel, "prep", [((16, BLOCK1, 128), BF16)], *inputs, scratch=scratch, space=pl.ANY, first=pl.ANY, vmem_mib=60
    )
    groups1 = [
        [((n // 4) * 2 + core) * 4 + n % 4 for n in names]
        for core, names in enumerate(listed(ORDER1))
    ]
    got1 = lax.all_to_all(
        block1, ("y", "core", "scen"), 0, 0, axis_index_groups=groups1, tiled=True
    )

    wide = lodf.astype(F32)
    terms = wide[None, :, :] * out_flow[:, None, :]
    screened = jnp.maximum(
        jnp.abs(flow_t + jnp.max(terms, axis=2)), jnp.abs(flow_t + jnp.min(terms, axis=2))
    )
    first = 512 * lax.axis_index("y") + 64 * lax.axis_index("scen")
    own_t = jnp.concatenate(
        [lax.dynamic_slice_in_dim(ptdf_out, first + 256 * i, 64, 1) for i in range(2)], axis=1
    ).T

    got1, own_t, screened = lax.optimization_barrier((got1, own_t, screened))
    other1 = lax.ppermute(got1, "core", [(0, 1), (1, 0)])
    part, sums = call(first_kernel, "first", [((128, 512), F32), ((8, 128), F32)], got1)
    block2 = call(
        second_kernel,
        "second",
        [((8, BLOCK2, 128), BF16)],
        other1, part, sums, ptdf_out, own_t, screened,
    )
    groups2 = [[c * 2 + core for c in names] for core, names in enumerate(listed(ORDER2))]
    got2 = lax.all_to_all(
        block2, ("cont", "core"), 0, 0, axis_index_groups=groups2, tiled=True
    )
    turned, direct, worst_part = call(
        combine_kernel,
        "combine",
        [((144, 128), I16), ((128, 128), F32), ((8, 128), F32)],
        got2, got1, other1, ratings,
        scratch=[pltpu.VMEM((128, 8), F32)],
    )

    def index(c, y, core, q):
        return ((c * sizes[1] + y) * sizes[2] + core) * sizes[3] + q

    pairs = [
        (index(c, y, core, q), index(c, y ^ (core * 2 + c // 4), core, q ^ (c % 4)))
        for c in range(sizes[0])
        for y in range(sizes[1])
        for core in range(sizes[2])
        for q in range(sizes[3])
    ]
    turned = lax.ppermute(turned, EVERY, pairs)
    block3 = call(
        functools.partial(finish_kernel, scale),
        "finish",
        [((16, BLOCK3, 128), I16)],
        turned, direct, worst_part,
    )
    group3 = sorted(range(16), key=lambda n: spot3(n // 2, n % 2))
    got3 = lax.all_to_all(
        block3, ("cont", "core"), 0, 0, axis_index_groups=[group3], tiled=True
    )
    schur, worst_t = call(
        place_kernel,
        "place",
        [((64, 2048), F32), ((64, 128), F32)],
        got3,
    )
    return worst_t.T, schur


def solution(mesh):
    n_cont, n_line, n_scen = (mesh.shape[a] for a in ("cont", "line", "scen"))
    fine = Mesh(mesh.devices.reshape(n_cont, n_line // 2, 2, n_scen), EVERY)
    line = ("y", "core")
    every = P(EVERY)
    in_specs = (
        P(line, "cont"),
        P(line, "scen"),
        P("scen", "cont"),
        P(line),
        P(line, None),
        P("cont", None),
        every,
        every,
        every,
        every,
    )
    out_specs = (P(line, "scen"), P((*line, "scen"), None))
    return jax.shard_map(local, mesh=fine, in_specs=in_specs, out_specs=out_specs, check_vma=False)
```

```python
import functools

import jax
import jax.numpy as jnp
from jax import lax
from jax.experimental import pallas as pl
from jax.experimental.pallas import tpu as pltpu
from jax.sharding import Mesh
from jax.sharding import PartitionSpec as P


F32 = jnp.float32
BF16 = jnp.bfloat16
I16 = jnp.int16

M_OWN = 0
M_TILE = 32
LIST = 64
BLOCK1 = 96

TAIL2 = 128
BLOCK2 = 160

BLOCK3 = 80


def iota(shape, axis):
    return lax.broadcasted_iota(jnp.int32, shape, axis)


def dot(a, b, dims):
    return lax.dot_general(a, b, (dims, ((), ())), preferred_element_type=F32)


NN = ((1,), (0,))
NT = ((1,), (1,))
TN = ((0,), (0,))


def split(x):
    high = x.astype(BF16)
    return high, (x - high.astype(F32)).astype(BF16)


def split3(x):
    high = x.astype(BF16)
    rest = x - high.astype(F32)
    mid, low = split(rest)
    return high, mid, low


ORDER1 = (16, False, 15)
ORDER2 = (8, False, 4)
ORDER3 = (8, False, 0, True)


def spot(order, n, core):
    size, reverse, other = order[:3]
    bits = size.bit_length() - 1
    if reverse:
        n = sum(((n >> i) & 1) << (bits - 1 - i) for i in range(bits))
    return n ^ (other * core) if other else n


def spot3(c, core):
    at = spot(ORDER3, c, core)
    return core * 8 + at if ORDER3[3] else at * 2 + core


def listed(order):
    names = [sorted(range(order[0]), key=lambda n: spot(order, n, core)) for core in range(2)]
    return names


def place():
    return tuple(lax.axis_index(a) for a in ("cont", "y", "core", "scen"))


def prep_kernel(*refs):
    hbm, out, local, sems = refs[:9], refs[9], refs[10:19], refs[19]
    block, out_sems = refs[20], refs[21]
    c, y, core, q = place()
    lines_here = pl.ds(pl.multiple_of(q * 32, 32), 32)
    copies = []
    for i, (source, target) in enumerate(zip(hbm, local)):
        source = source.at[lines_here, :] if i == 8 else source
        copies.append(pltpu.make_async_copy(source, target, sems.at[i]))
    for copy in copies[8:] + copies[:8]:
        copy.start()
    used, k4, l4, s4, lodf, flow, out_flow, limits, own_ref = local
    copies[8].wait()
    own = own_ref[...]
    for yy in range(4):
        for qq in range(4):
            first = 512 * yy + 64 * qq
            part = jnp.concatenate(
                [own[:, first : first + 64], own[:, first + 256 : first + 320]], axis=1
            )
            block[spot(ORDER1, yy * 4 + qq, core), M_OWN : M_OWN + 32, :] = part
            for cc in range(2):
                to_y = lax.bitwise_xor(jnp.int32(yy), 2 * cc + c // 4)
                to = to_y * 4 + lax.bitwise_xor(jnp.int32(qq), c % 4)
                lines = jnp.where(to < yy * 4 + qq, part[0:16].astype(F32), part[16:32].astype(F32))
                first_row = M_TILE + 16 * cc
                block[spot(ORDER1, to, core), first_row : first_row + 16, :] = lines.astype(BF16)
    mon_out = pltpu.make_async_copy(
        block.at[:, 0:LIST, :], out.at[:, 0:LIST, :], out_sems.at[0]
    )
    mon_out.start()
    for copy in copies[:8]:
        copy.wait()
    n = 512

    def row(ref):
        return jnp.concatenate([ref[j : j + 1, :] for j in range(4)], axis=1)

    k, l, s = row(k4), row(l4), row(s4)
    lines, conts = lodf.shape
    scens = flow.shape[0]
    is_l = iota((lines, n), 0) == l
    is_s = iota((scens, n), 0) == s
    one_l = jnp.where(is_l, 1.0, 0.0).astype(BF16)
    one_k = jnp.where(iota((conts, n), 0) == k, 1.0, 0.0).astype(BF16)
    by_k = dot(jnp.concatenate([lodf[...], *split3(out_flow[...])], axis=0), one_k, NN)
    coef = jnp.sum(jnp.where(is_l, by_k[:lines], 0.0), axis=0, keepdims=True)
    outs = by_k[lines : lines + scens] + by_k[lines + scens : lines + 2 * scens]
    outs = outs + by_k[lines + 2 * scens :]
    outs = jnp.sum(jnp.where(is_s, outs, 0.0), axis=0, keepdims=True)
    ratings = jnp.broadcast_to(limits[...], (16, lines))
    by_l = dot(jnp.concatenate([*split3(flow[...]), *split3(ratings)], axis=0), one_l, NN)
    flows = by_l[:scens] + by_l[scens : 2 * scens] + by_l[2 * scens : 3 * scens]
    flows = jnp.sum(jnp.where(is_s, flows, 0.0), axis=0, keepdims=True)
    base = 3 * scens
    rating = by_l[base : base + 1] + by_l[base + 16 : base + 17] + by_l[base + 32 : base + 33]
    ratio = (flows + coef * outs) / rating
    weight = jnp.where(iota((1, n), 1) < used[0], 1.0 + ratio * ratio, 0.0)
    mixed = weight * coef
    square = mixed * coef

    def rows16(x):
        parts = [p.astype(F32) for p in split3(x)]
        return jnp.concatenate([*parts, jnp.zeros((13, n), F32)], axis=0).astype(BF16)

    e_parts = dot(rows16(square), one_k, NT)
    e_sum = e_parts[0:1] + e_parts[1:2] + e_parts[2:3]
    d_parts = dot(rows16(weight), one_l, NT)
    d_sum = d_parts[0:1] + d_parts[1:2] + d_parts[2:3]

    upper = k >= conts // 2
    kl = jnp.where(upper, k - conts // 2, k)
    fields = [
        l.astype(F32),
        kl.astype(F32),
        jnp.where(upper, 0.0, mixed),
        jnp.where(upper, mixed, 0.0),
        *[p.astype(F32) for p in split(e_sum)],
    ]
    rows = [f[:, 128 * j : 128 * j + 128] for f in fields for j in range(4)]
    rows += [p.astype(F32) for p in split(d_sum)]
    rows += [jnp.zeros((32 - len(rows), 128), F32)]
    table = jnp.concatenate(rows, axis=0).astype(BF16)
    for b in range(16):
        block[b, LIST : LIST + 32, :] = table
    lists_out = pltpu.make_async_copy(
        block.at[:, LIST:BLOCK1, :], out.at[:, LIST:BLOCK1, :], out_sems.at[1]
    )
    lists_out.start()
    mon_out.wait()
    lists_out.wait()


def half_product(got, core):
    def at(n):
        return spot(ORDER1, n, core)

    def pieces(f, j):
        l, kl, low, up = f[j : j + 1], f[4 + j : 5 + j], f[8 + j : 9 + j], f[12 + j : 13 + j]
        is_l = iota((128, 128), 0).astype(F32) == l
        left = jnp.concatenate(
            [jnp.where(is_l, low, 0.0), jnp.where(is_l, up, 0.0)], axis=0
        ).astype(BF16)
        right = jnp.where(iota((256, 128), 0).astype(F32) == kl, 1.0, 0.0).astype(BF16)
        return left, right

    e_sum, d_rows, cores = jnp.zeros((8, 128), F32), [], []
    for yy in range(4):
        tables = [got[at(yy * 4 + r), LIST : LIST + 32, :].astype(F32) for r in range(4)]
        both = [pieces(f, j) for f in tables for j in range(4)]
        blocks = dot(
            jnp.concatenate([p[0] for p in both], axis=1),
            jnp.concatenate([p[1] for p in both], axis=1),
            NT,
        )
        cores.append(jnp.concatenate([blocks[:128], blocks[128:]], axis=1))
        total = tables[0] + tables[1] + tables[2] + tables[3]
        e_sum = e_sum + total[16:24]
        d_rows.append(total[24:25] + total[25:26])
    mon = jnp.concatenate([got[at(i), M_OWN : M_OWN + 32, :] for i in range(16)], axis=0)
    high, low = split(jnp.concatenate(cores, axis=0))
    part = dot(mon, high, TN) + dot(mon, low, TN)
    return part, jnp.concatenate([e_sum[0:4] + e_sum[4:8], *d_rows], axis=0)


def first_kernel(got, part, sums):
    part[...], sums[...] = half_product(got, lax.axis_index("core"))


def second_kernel(got, part1, sums1, out_rows, own_t, screened, sent):
    c, y, core, q = place()
    part, sums = half_product(got, 1 - core)
    e_sum = sums1[0:4, :] + sums[0:4]
    e_row = jnp.concatenate([e_sum[j : j + 1] for j in range(4)], axis=1)
    part = part1[...] + part + (0.5 * e_row) * own_t[...].astype(F32)
    left = jnp.concatenate(split(part), axis=0)
    d_all = jnp.concatenate([sums1[4:8, :], sums[4:8]], axis=0)
    d_rows = [p.astype(F32) for p in split(d_all)]
    for i in range(8):
        w_rows = [p.astype(F32) for p in split(screened[8 * i : 8 * i + 8, :])]
        sent[spot(ORDER2, i, core), TAIL2:BLOCK2, :] = jnp.concatenate([*w_rows, *d_rows], axis=0).astype(BF16)
    half = lax.bitwise_xor(y // 2, core)
    for yy in range(2):
        first = pl.multiple_of(half * 1024 + 512 * yy, 512)
        both = dot(left, out_rows[:, pl.ds(first, 512)], NN)
        tile = (both[:128] + both[128:]).astype(BF16)
        for qq in range(4):
            to = lax.bitwise_xor(jnp.int32(yy), y % 2) * 4 + lax.bitwise_xor(jnp.int32(qq), q)
            sent[spot(ORDER2, to, core), 0:128, :] = jnp.concatenate(
                [tile[:, 64 * qq : 64 * qq + 64], tile[:, 256 + 64 * qq : 320 + 64 * qq]], axis=1
            )


def encode(x):
    top = jnp.maximum(jnp.max(jnp.abs(x), axis=0, keepdims=True), 1e-30)
    exponent = jnp.floor(jnp.log2(top) + 1.001) - 15.0
    return jnp.floor(x * jnp.exp2(-exponent) + 0.5), exponent


def decode(code, exponent):
    return code * jnp.exp2(exponent)


def combine_kernel(got2, own, other, limits, turned, direct, worst, d_ref):
    c, y, core, q = place()
    a = got2[0, 0:128, :].astype(F32)
    tail = got2[0, TAIL2:BLOCK2, :].astype(F32)
    high = tail[0:8] + tail[8:16]
    d_all = tail[16:24] + tail[24:32]
    for i in range(1, 8):
        a = a + got2[i, 0:128, :].astype(F32)
        tail = got2[i, TAIL2:BLOCK2, :].astype(F32)
        high = jnp.maximum(high, tail[0:8] + tail[8:16])
        d_all = d_all + (tail[16:24] + tail[24:32])
    worst[...] = high / limits[...]
    d_ref[...] = d_all.T

    def side(h):
        lefts = []
        for i, got in enumerate((own, other)):
            for yy in range(4):
                for r in range(4):
                    lines = pl.ds(pl.multiple_of(32 * r + 16 * h, 16), 16)
                    n = spot(ORDER1, yy * 4 + r, core if i == 0 else 1 - core)
                    mon = got[n, pl.ds(pl.multiple_of(M_OWN + 16 * h, 16), 16), :]
                    scaled = mon.astype(F32) * d_ref[lines, 4 * i + yy : 4 * i + yy + 1]
                    lefts.append(jnp.concatenate(split(scaled), axis=1))
        return jnp.concatenate(lefts, axis=0)

    def write(both, factor):
        total = a + factor * (both[:128] + both[128:])
        direct[...] = total
        code, exp = encode(total.T)
        rows = [code, exp, jnp.zeros((15, 128), F32)]
        turned[...] = jnp.concatenate(rows, axis=0).astype(jnp.int32).astype(I16)

    alone = (c == 0) & (core == 0)

    @pl.when(alone)
    def _():
        both = 0.0
        for h in range(2):
            rights = [
                g[spot(ORDER1, n, k), M_OWN + 16 * h : M_OWN + 16 * h + 16, :]
                for g, k in ((own, core), (other, 1 - core))
                for n in range(16)
            ]
            both = both + dot(side(h), jnp.concatenate(rights, axis=0), TN)
        write(both, 0.5)

    @pl.when(jnp.logical_not(alone))
    def _():
        to_y = lax.bitwise_xor(y, 2 * core + c // 4)
        to_q = lax.bitwise_xor(q, c % 4)
        h = jnp.where(y * 4 + q < to_y * 4 + to_q, 0, 1)
        there = pl.ds(pl.multiple_of(M_TILE + 16 * core, 16), 16)
        rights = [
            g[spot(ORDER1, n, k), there, :]
            for g, k in ((own, core), (other, 1 - core))
            for n in range(16)
        ]
        write(dot(side(h), jnp.concatenate(rights, axis=0), TN), 1.0)


def finish_kernel(scale, turned, direct, worst, sent):
    other = turned[...].astype(jnp.int32).astype(F32)
    tile = (direct[...] + decode(other[:128], other[128:129])) * scale
    worst_code, worst_exp = encode(worst[...])
    for core in range(2):
        code, exp = encode(tile[64 * core : 64 * core + 64, :])
        rows = [code, worst_code, exp, worst_exp, jnp.zeros((BLOCK3 - 74, 128), F32)]
        block = jnp.concatenate(rows, axis=0).astype(jnp.int32).astype(I16)
        for i in range(8):
            sent[spot3(i, core), :, :] = block


def place_kernel(got, schur, worst):
    c, y, core, q = place()
    for yy in range(4):
        parts = []
        for qq in range(4):
            source_c = lax.bitwise_xor(jnp.int32(yy % 2), y % 2) * 4
            source_c = source_c + lax.bitwise_xor(jnp.int32(qq), q)
            source_core = lax.bitwise_xor(jnp.int32(yy // 2), y // 2)
            parts.append(got[spot3(source_c, source_core), :, :])
        block = jnp.concatenate([p[:, :64] for p in parts] + [p[:, 64:] for p in parts], axis=1)
        block = block.astype(jnp.int32).astype(F32)
        schur[:, 512 * yy : 512 * yy + 512] = decode(block[0:64], block[72:73])
    for i in range(8):
        block = got[spot3(i, core), 64:80, :].astype(jnp.int32).astype(F32)
        worst[8 * i : 8 * i + 8, :] = decode(block[0:8], block[9:10])


def call(kernel, name, outs, *args, scratch=(), space=pltpu.VMEM, first=pltpu.VMEM, vmem_mib=24):
    vmem = pl.BlockSpec(memory_space=pltpu.VMEM)
    specs = [pl.BlockSpec(memory_space=first)] + [vmem] * (len(outs) - 1)
    shapes = [jax.ShapeDtypeStruct(s, d) for s, d in outs]
    many = len(outs) > 1
    return pl.pallas_call(
        kernel,
        name=name,
        out_shape=shapes if many else shapes[0],
        in_specs=[pl.BlockSpec(memory_space=space)] * len(args),
        out_specs=specs if many else specs[0],
        scratch_shapes=list(scratch),
        compiler_params=pltpu.CompilerParams(vmem_limit_bytes=vmem_mib * 1024 * 1024),
    )(*args)


EVERY = ("cont", "y", "core", "scen")


def local(
    lodf, flow, out_flow, limits, ptdf_mon, ptdf_out, viol_cont, viol_line, viol_scen, rows_used
):
    sizes = [lax.axis_size(a) for a in EVERY]
    n_rows = viol_cont.shape[0]
    scale = 1.0 / (n_rows * sizes[0] * sizes[1] * sizes[2] * sizes[3])
    ratings = limits.reshape(1, -1)
    flow_t = flow.T

    inputs = [
        rows_used,
        viol_cont.reshape(4, 128),
        viol_line.reshape(4, 128),
        viol_scen.reshape(4, 128),
        lodf,
        flow_t,
        out_flow,
        ratings,
        ptdf_mon,
    ]
    scratch = [pltpu.SMEM(rows_used.shape, jnp.int32)]
    scratch += [pltpu.VMEM(a.shape, a.dtype) for a in inputs[1:8]]
    scratch += [pltpu.VMEM((32, ptdf_mon.shape[1]), BF16), pltpu.SemaphoreType.DMA((9,))]
    scratch += [pltpu.VMEM((16, BLOCK1, 128), BF16), pltpu.SemaphoreType.DMA((2,))]
    block1 = call(
        prep_kernel, "prep", [((16, BLOCK1, 128), BF16)], *inputs, scratch=scratch, space=pl.ANY, first=pl.ANY, vmem_mib=60
    )
    groups1 = [
        [((n // 4) * 2 + core) * 4 + n % 4 for n in names]
        for core, names in enumerate(listed(ORDER1))
    ]
    got1 = lax.all_to_all(
        block1, ("y", "core", "scen"), 0, 0, axis_index_groups=groups1, tiled=True
    )

    wide = lodf.astype(F32)
    terms = wide[None, :, :] * out_flow[:, None, :]
    screened = jnp.maximum(
        jnp.abs(flow_t + jnp.max(terms, axis=2)), jnp.abs(flow_t + jnp.min(terms, axis=2))
    )
    first = 512 * lax.axis_index("y") + 64 * lax.axis_index("scen")
    own_t = jnp.concatenate(
        [lax.dynamic_slice_in_dim(ptdf_out, first + 256 * i, 64, 1) for i in range(2)], axis=1
    ).T

    got1, own_t, screened = lax.optimization_barrier((got1, own_t, screened))
    other1 = lax.ppermute(got1, "core", [(0, 1), (1, 0)])
    part, sums = call(first_kernel, "first", [((128, 512), F32), ((8, 128), F32)], got1)
    block2 = call(
        second_kernel,
        "second",
        [((8, BLOCK2, 128), BF16)],
        other1, part, sums, ptdf_out, own_t, screened,
    )
    groups2 = [[c * 2 + core for c in names] for core, names in enumerate(listed(ORDER2))]
    got2 = lax.all_to_all(
        block2, ("cont", "core"), 0, 0, axis_index_groups=groups2, tiled=True
    )
    turned, direct, worst_part = call(
        combine_kernel,
        "combine",
        [((144, 128), I16), ((128, 128), F32), ((8, 128), F32)],
        got2, got1, other1, ratings,
        scratch=[pltpu.VMEM((128, 8), F32)],
    )

    def index(c, y, core, q):
        return ((c * sizes[1] + y) * sizes[2] + core) * sizes[3] + q

    pairs = [
        (index(c, y, core, q), index(c, y ^ (core * 2 + c // 4), core, q ^ (c % 4)))
        for c in range(sizes[0])
        for y in range(sizes[1])
        for core in range(sizes[2])
        for q in range(sizes[3])
    ]
    turned = lax.ppermute(turned, EVERY, pairs)
    block3 = call(
        functools.partial(finish_kernel, scale),
        "finish",
        [((16, BLOCK3, 128), I16)],
        turned, direct, worst_part,
    )
    group3 = sorted(range(16), key=lambda n: spot3(n // 2, n % 2))
    got3 = lax.all_to_all(
        block3, ("cont", "core"), 0, 0, axis_index_groups=[group3], tiled=True
    )
    schur, worst_t = call(
        place_kernel,
        "place",
        [((64, 2048), F32), ((64, 128), F32)],
        got3,
    )
    return worst_t.T, schur


def solution(mesh):
    n_cont, n_line, n_scen = (mesh.shape[a] for a in ("cont", "line", "scen"))
    fine = Mesh(mesh.devices.reshape(n_cont, n_line // 2, 2, n_scen), EVERY)
    line = ("y", "core")
    every = P(EVERY)
    in_specs = (
        P(line, "cont"),
        P(line, "scen"),
        P("scen", "cont"),
        P(line),
        P(line, None),
        P("cont", None),
        every,
        every,
        every,
        every,
    )
    out_specs = (P(line, "scen"), P((*line, "scen"), None))
    return jax.shard_map(local, mesh=fine, in_specs=in_specs, out_specs=out_specs, check_vma=False)
```
